32 devices in a mesh: dp: 8 (over z, y), tensor: 4 (over x, core).
Axes of the slice: x: 2, y: 2, z: 4, core: 2. Of those that a mesh axis runs over, the one named last changes fastest.
Arguments:
- tokens: bfloat16 [336, 96, 512], P('tensor', 'dp'), may hold values from -6 to 6
- seq_counts: int32 [8], P('dp'), may hold values from 1 to 12, as said below
- first_frame: int32 [96], P('dp'), may hold values from 0 to 5
- norm1_gain: float32 [512], replicated, may hold values from 0.5 to 1.5
- norm1_bias: float32 [512], replicated, may hold values from -2 to 2
- qkv_weight: bfloat16 [512, 1536], P(None, 'tensor'), may hold values from -0.25 to 0.25
- out_weight: bfloat16 [512, 512], P('tensor'), may hold values from -2 to 2
- out_bias: float32 [512], replicated, may hold values from -2 to 2
- norm2_gain: float32 [512], replicated, may hold values from 0.5 to 1.5
- norm2_bias: float32 [512], replicated, may hold values from -2 to 2
- up_weight: bfloat16 [512, 2048], P(None, 'tensor'), may hold values from -0.25 to 0.25
- up_bias: float32 [2048], P('tensor'), may hold values from -2 to 2
- down_weight: bfloat16 [2048, 512], P('tensor'), may hold values from -0.125 to 0.125
- down_bias: float32 [512], replicated, may hold values from -2 to 2
- out_cotangent: bfloat16 [336, 96, 512], P('tensor', 'dp'), may hold values from -6 to 6
Outputs:
- block_output: bfloat16 [336, 96, 512], P('tensor', 'dp')
- input_grad: bfloat16 [336, 96, 512], P('tensor', 'dp')
- qkv_weight_grad: float32 [512, 1536], P(None, 'tensor')
- out_weight_grad: float32 [512, 512], P('tensor')
- up_weight_grad: float32 [512, 2048], P(None, 'tensor')
- down_weight_grad: float32 [2048, 512], P('tensor')
- up_bias_grad: float32 [2048], P('tensor')
- out_bias_grad: float32 [512], replicated
- down_bias_grad: float32 [512], replicated
- norm1_gain_grad: float32 [512], replicated
- norm1_bias_grad: float32 [512], replicated
- norm2_gain_grad: float32 [512], replicated
- norm2_bias_grad: float32 [512], replicated
The draws below stay inside these ranges and needn't reach their ends.
Inputs may be any that keep to these rules, and one draw needn't show every extreme that they name: `seq_counts`: entry i is how many of the first sequence slots of data index i are live, out of 12; some index is full in every draw.
All inputs are finite; a program needn't handle non-finite values.
Results may differ from the reference program's by a relative error of at most 0.02.
Values may be sent and summed in bfloat16 or wider, within the bound.
No kernel may reach another device: no remote copies, remote signals or barrier semaphores. Data moves between devices by JAX's collectives and lax.ppermute only.
A program may use at most 192 MiB of HBM per device.

```python
import jax
import jax.numpy as jnp
from jax import lax

D = 512
H = 8
HD = 64
FF = 2048
FRAMES = 6
FRAME_TOK = 56
SEQ_LEN = 336
SEQ_DEV = 12
SEQS = 96
N_DP = 8
N_TENSOR = 4


def draw_seq_counts(key, part):
    key = jax.random.fold_in(key, 11)
    key_level, key_full = jax.random.split(key)
    levels = jax.random.randint(key_level, (N_DP,), 1, SEQ_DEV + 1)
    full_index = jax.random.randint(key_full, (), 0, N_DP)
    counts = jnp.where(jnp.arange(N_DP) == full_index, SEQ_DEV, levels)
    return counts.astype(jnp.int32)


def place_ends(array, stream_key, least, top_value):
    longest = array.shape.index(max(array.shape))
    spots = []
    for shift in (0, 1):
        where = [jax.random.randint(jax.random.fold_in(stream_key, axis), (), 0, length) for axis, length in enumerate(array.shape)]
        where[longest] = (where[longest] + shift) % array.shape[longest]
        spots.append(tuple(where))
    return array.at[spots[0]].set(least).at[spots[1]].set(top_value)


def shard_levels(stream_key, extent, cuts, least, top_value):
    loudness, own = 1.0, jax.random.fold_in(stream_key, 6)
    for position, blocks in cuts:
        steps = jnp.exp(jax.random.uniform(jax.random.fold_in(own, position), (blocks,), jnp.float32, least / len(cuts), top_value / len(cuts)))
        loudness = loudness * jnp.repeat(steps, extent[position] // blocks).reshape([-1 if axis == position else 1 for axis in range(len(extent))])
    return loudness


def bell_draw(rng, dims, scale, limit, cuts=(), kind=jnp.bfloat16):
    array = scale * jax.random.normal(rng, dims, jnp.float32)
    if cuts:
        array = array * shard_levels(rng, dims, cuts, -0.22, 0.18)
    return jnp.clip(array, -limit, limit).astype(kind)


def setup_inputs(seed: int = 0) -> dict:
    key_of = jax.random.split(jax.random.key(seed), 16)
    tokens = bell_draw(key_of[0], (SEQ_LEN, SEQS, D), 1.0, 6.0, ((0, 4), (1, 8)))
    seq_counts = draw_seq_counts(jax.random.fold_in(key_of[15], 71), 0)
    first_frame = place_ends(jax.random.randint(key_of[2], (SEQS,), 0, FRAMES), jax.random.fold_in(key_of[2], 1), 0, FRAMES - 1).astype(jnp.int32)
    norm1_gain = jnp.clip(1.0 + 0.1 * jax.random.normal(key_of[3], (D,), jnp.float32), 0.5, 1.5)
    norm1_bias = bell_draw(key_of[4], (D,), 0.3, 2.0, (), jnp.float32)
    qkv_weight = bell_draw(key_of[5], (D, 3 * H * HD), D ** -0.5, 0.25, ((1, 4),))
    out_weight = bell_draw(key_of[6], (H * HD, D), (max(H * HD // 64, 1)) ** -0.5, 2.0, ((0, 4),))
    out_bias = bell_draw(key_of[7], (D,), 0.3, 2.0, (), jnp.float32)
    norm2_gain = jnp.clip(1.0 + 0.1 * jax.random.normal(key_of[8], (D,), jnp.float32), 0.5, 1.5)
    norm2_bias = bell_draw(key_of[9], (D,), 0.3, 2.0, (), jnp.float32)
    up_weight = bell_draw(key_of[10], (D, FF), D ** -0.5, 0.25, ((1, 4),))
    up_bias = bell_draw(key_of[11], (FF,), 0.3, 2.0, ((0, 4),), jnp.float32)
    down_weight = bell_draw(key_of[12], (FF, D), FF ** -0.5, 0.125, ((0, 4),))
    down_bias = bell_draw(key_of[13], (D,), 0.3, 2.0, (), jnp.float32)
    out_cotangent = bell_draw(key_of[14], (SEQ_LEN, SEQS, D), 1.0, 6.0, ((0, 4), (1, 8)))
    return dict(tokens=tokens, seq_counts=seq_counts, first_frame=first_frame, norm1_gain=norm1_gain, norm1_bias=norm1_bias, qkv_weight=qkv_weight, out_weight=out_weight, out_bias=out_bias, norm2_gain=norm2_gain, norm2_bias=norm2_bias, up_weight=up_weight, up_bias=up_bias, down_weight=down_weight, down_bias=down_bias, out_cotangent=out_cotangent)


@jax.custom_vjp
def low(v):
    return lax.optimization_barrier(v.astype(jnp.bfloat16)).astype(jnp.float32)

@jax.custom_vjp
def low_back(v):
    return v

def low_keep(v):
    return (low(v), None)

def low_pass(kept, grad):
    return (grad,)

def back_keep(v):
    return (v, None)

def back_low(kept, grad):
    return (low(grad),)
low.defvjp(low_keep, low_pass)
low_back.defvjp(back_keep, back_low)

def layer_norm(values, gain, bias):
    centered = values - lax.optimization_barrier(jnp.mean(values, axis=-1, keepdims=True))
    spread = lax.optimization_barrier(jnp.mean(centered * centered, axis=-1, keepdims=True))
    return centered * lax.rsqrt(spread + 1e-05) * gain + bias

def forward(residual_in, params, frames, live):
    g1, b1, wqkv, wo, bo, g2, b2, wup, bup, wdown, bdown = params
    hp = lax.Precision.HIGHEST
    length = residual_in.shape[0]
    batch = residual_in.shape[1]
    groups = N_TENSOR
    local_heads = H // groups
    local_ff = FF // groups
    a_one = low(layer_norm(residual_in, g1, b1))
    a_one_t = low_back(jnp.broadcast_to(a_one[:, :, None, :], (length, batch, groups, D)))
    qkv = jnp.einsum('pbtd,dte->pbte', a_one_t, wqkv.reshape(D, groups, local_heads * 3 * HD), precision=hp)
    qkv = low(low_back(qkv)).reshape(length, batch, H, 3, HD)
    queries = qkv[:, :, :, 0]
    keys = qkv[:, :, :, 1]
    values = qkv[:, :, :, 2]
    positions = jnp.arange(length)
    causal = positions[None, :] <= positions[:, None]
    diagonal = positions[None, :] == positions[:, None]
    starts = (frames * FRAME_TOK)[:, None, None]
    allowed = causal[None] & ((positions[None, None, :] >= starts) | diagonal[None])
    allowed = allowed[:, None]
    raw_scores = low_back(jnp.einsum('pbhe,qbhe->bhpq', queries, keys, precision=hp) * HD ** (-0.5))
    masked = jnp.where(allowed, raw_scores, -1e+30)
    row_top = lax.optimization_barrier(jnp.max(masked, axis=-1, keepdims=True))
    exponent = jnp.exp(masked - row_top)
    probs = low(exponent / lax.optimization_barrier(jnp.sum(exponent, axis=-1, keepdims=True)))
    attended = jnp.einsum('bhpq,qbhe->pbhe', probs, values, precision=hp)
    attended = low(low_back(attended)).reshape(length, batch, groups, local_heads * HD)
    parts = jnp.einsum('pbte,ted->pbtd', attended, wo.reshape(groups, local_heads * HD, D), precision=hp)
    attn = low_back(lax.optimization_barrier(jnp.sum(low(parts), axis=2)) + bo)
    after_attn = residual_in + attn
    a_two = low(layer_norm(after_attn, g2, b2))
    a_two_t = low_back(jnp.broadcast_to(a_two[:, :, None, :], (length, batch, groups, D)))
    pre_act = jnp.einsum('pbtd,dtf->pbtf', a_two_t, wup.reshape(D, groups, local_ff), precision=hp)
    pre_act = low_back(pre_act + bup.reshape(groups, local_ff))
    hidden = low(jax.nn.gelu(pre_act, approximate=True))
    parts = jnp.einsum('pbtf,tfd->pbtd', hidden, wdown.reshape(groups, local_ff, D), precision=hp)
    mlp = low_back(lax.optimization_barrier(jnp.sum(low(parts), axis=2)) + bdown)
    return live[None, :, None] * (after_attn + mlp)

def reference(tokens, seq_counts, first_frame, norm1_gain, norm1_bias, qkv_weight, out_weight, out_bias, norm2_gain, norm2_bias, up_weight, up_bias, down_weight, down_bias, out_cotangent):
    params = tuple((arr.astype(jnp.float32) for arr in (norm1_gain, norm1_bias, qkv_weight, out_weight, out_bias, norm2_gain, norm2_bias, up_weight, up_bias, down_weight, down_bias)))
    blocks_in = tokens.astype(jnp.float32).reshape(SEQ_LEN, N_DP, SEQ_DEV, D).transpose(1, 0, 2, 3)
    blocks_cot = out_cotangent.astype(jnp.float32).reshape(SEQ_LEN, N_DP, SEQ_DEV, D).transpose(1, 0, 2, 3)
    frames = first_frame.reshape(N_DP, SEQ_DEV).astype(jnp.int32)
    live = (jnp.arange(SEQ_DEV, dtype=jnp.int32)[None, :] < seq_counts.astype(jnp.int32)[:, None]).astype(jnp.float32)

    def accumulate(totals, block):
        block_in, block_cot, block_frames, block_live = block
        result, pullback = jax.vjp(lambda inner, weights: forward(inner, weights, block_frames, block_live), block_in, params)
        grad_in, grad_params = pullback(block_cot)
        totals = jax.tree.map(lambda left, right: left + right, totals, grad_params)
        return (totals, (result, grad_in))
    zeros = jax.tree.map(jnp.zeros_like, params)
    grads, (results, grads_in) = lax.scan(accumulate, zeros, (blocks_in, blocks_cot, frames, live))
    block_output = results.transpose(1, 0, 2, 3).reshape(SEQ_LEN, SEQS, D).astype(jnp.bfloat16)
    input_grad = grads_in.transpose(1, 0, 2, 3).reshape(SEQ_LEN, SEQS, D).astype(jnp.bfloat16)
    dg1, db1, dwqkv, dwo, dbo, dg2, db2, dwup, dbup, dwdown, dbdown = grads
    return (block_output, input_grad, dwqkv, dwo, dwup, dwdown, dbup, dbo, dbdown, dg1, db1, dg2, db2)
```

```python
import functools
import math

import jax
import jax.numpy as jnp
from jax import lax
from jax.experimental import pallas as pl
from jax.experimental.pallas import tpu as pltpu
from jax.sharding import PartitionSpec as P

HD = 64
FRAME_TOK = 56
BF16 = jnp.bfloat16
F32 = jnp.float32
NN = (((1,), (0,)), ((), ()))
NT = (((1,), (1,)), ((), ()))
TN = (((0,), (0,)), ((), ()))
GELU_A = 0.7978845608
GELU_B = 0.044715
VMEM_LIMIT = 56 << 20


def dot(a, b, dims=NN):
    return lax.dot_general(a, b, dims, preferred_element_type=F32)


def stats(x):
    c = x - jnp.mean(x, axis=-1, keepdims=True)
    inv = lax.rsqrt(jnp.mean(c * c, axis=-1, keepdims=True) + 1e-5)
    return c * inv, inv


def norm_back(d, hat, inv, gain):
    e = d * gain
    return inv * (
        e - jnp.mean(e, axis=-1, keepdims=True) - hat * jnp.mean(e * hat, axis=-1, keepdims=True)
    )


def full(a):
    return pl.BlockSpec(a.shape, lambda *_: (0,) * len(a.shape))


def struct(shape, dtype):
    return jax.ShapeDtypeStruct(shape, dtype)


def call(kernel, scalars, args, out_shape, grid=(1,), in_specs=None, out_specs=None, scratch=(), flops=0, name=None, aliases=None):
    in_specs = [full(a) for a in args] if in_specs is None else in_specs
    out_specs = [full(o) for o in out_shape] if out_specs is None else out_specs
    moved = sum(math.prod(a.shape) * a.dtype.itemsize for a in (*args, *out_shape))
    return pl.pallas_call(
        kernel,
        grid_spec=pltpu.PrefetchScalarGridSpec(
            num_scalar_prefetch=len(scalars),
            grid=grid,
            in_specs=in_specs,
            out_specs=out_specs,
            scratch_shapes=list(scratch),
        ),
        out_shape=list(out_shape),
        compiler_params=pltpu.CompilerParams(vmem_limit_bytes=VMEM_LIMIT),
        cost_estimate=pl.CostEstimate(flops=flops, bytes_accessed=moved, transcendentals=0),
        name=name,
        input_output_aliases=aliases or {},
    )(*scalars, *args)


def pack_kernel(wqkv_ref, wout_ref, ub_ref, w_ref):
    d = wout_ref.shape[1]
    half = d // 2
    ub = ub_ref[...]
    high = ub.astype(BF16).astype(F32)
    row = lax.broadcasted_iota(jnp.int32, (16, d), 0)
    ub = jnp.where(row == 0, high, jnp.where(row == 1, ub - high, 0.0)).astype(BF16)
    side = wout_ref.shape[0]
    for h in range(2):
        here = pl.ds(h * half, half)
        a, b, c = (wqkv_ref[here, pl.ds(128 * j, 128)].astype(F32) for j in range(3))
        low = lax.broadcasted_iota(jnp.int32, a.shape, 1) < HD
        w_ref[h, 0:half, 0:128] = jnp.where(low, a, b).astype(BF16)
        w_ref[h, 0:half, 128:256] = pltpu.roll(jnp.where(low, c, a), HD, 1).astype(BF16)
        w_ref[h, 0:half, 256:384] = jnp.where(low, b, c).astype(BF16)
        for j in range(half // side):
            w_ref[h, pl.ds(j * side, side), 384:512] = wout_ref[:, pl.ds(h * half + 128 * j, 128)]
        w_ref[h, half:half + 16, :] = ub


def pack(wqkv, wout, ub):
    d = wqkv.shape[0]
    return call(pack_kernel, (), (wqkv, wout, ub), [struct((2, d // 2 + 16, d), BF16)], name="pack_weights")[0]


def place_kernel(me_ref, b0, b1, b2, b3, out_ref):
    each = b0.shape[0]
    for k, b in enumerate((b0, b1, b2, b3)):
        out_ref[pl.ds((me_ref[0] ^ k) * each, each)] = b[...]


def place(me, blocks):
    each, rows, d = blocks[0].shape
    return call(place_kernel, (me,), blocks, [struct((4 * each, rows, d), BF16)], name="place")[0]


def attn_fwd_kernel(me_ref, bit_ref, ff_ref, t0, t1, t2, t3, w0, w1, w2a, w2b, w3a, w3b,
                    g1_ref, b1_ref, bo_ref, g2_ref, b2_ref,
                    qkv_ref, p_ref, o_ref, x_ref, y1_ref, a1_ref, a2_ref, wq_ref, wo_ref, ub_ref,
                    blk_sc, bias_sc):
    s = pl.program_id(0)
    _, rows, d = t0.shape
    length = 4 * rows
    me = me_ref[0]

    @pl.when(s == 0)
    def _():
        bit = bit_ref[0]
        half = d // 2
        for k, parts in enumerate((
            ((0, w0.at[0]), (half, w0.at[1])),
            ((0, w1.at[0]), (half, w1.at[1])),
            ((pl.multiple_of(bit * half, half), w2a), (pl.multiple_of((1 - bit) * half, half), w2b)),
            ((pl.multiple_of(bit * half, half), w3a), (pl.multiple_of((1 - bit) * half, half), w3b)),
        )):
            for at, w in parts:
                wq_ref[pl.ds(at, half), pl.ds(384 * k, 384)] = w[0:half, 0:384]
                for j in range(half // 128):
                    lane = pl.multiple_of(at + 128 * j, 128)
                    wo_ref[pl.ds(128 * k, 128), pl.ds(lane, 128)] = w[pl.ds(128 * j, 128), 384:512]
            ub = parts[0][1][half:half + 16, :].astype(F32)
            ub_ref[k] = jnp.broadcast_to(ub[0:1] + ub[1:2], ub_ref.shape[1:])

    for k, t in enumerate((t0, t1, t2, t3)):
        blk_sc[me ^ k] = t[0].astype(F32)
    for i in range(4):
        x_ref[0, pl.ds(i * rows, rows), :] = blk_sc[i]
    hat, _ = stats(x_ref[0])
    a1 = (hat * g1_ref[...] + b1_ref[...]).astype(BF16)
    a1_ref[0] = a1
    qkv_ref[0] = dot(a1, wq_ref[...]).astype(BF16)
    start = ff_ref[me * pl.num_programs(0) + s] * FRAME_TOK
    jj = lax.broadcasted_iota(jnp.int32, (length, length), 0)
    ii = lax.broadcasted_iota(jnp.int32, (length, length), 1)
    bias_sc[...] = jnp.where((jj <= ii) & ((jj >= start) | (jj == ii)), 0.0, -1e30)
    lane = lax.broadcasted_iota(jnp.int32, (length, 128), 1)
    for p in range(4):
        q = qkv_ref[0, :, pl.ds(p * 384, 128)]
        k = qkv_ref[0, :, pl.ds(p * 384 + 128, 128)]
        v = qkv_ref[0, :, pl.ds(p * 384 + 256, 128)]
        acc = None
        for h in range(2):
            mine = (lane < HD) if h == 0 else (lane >= HD)
            kh = jnp.where(mine, k, jnp.zeros_like(k))
            vh = jnp.where(mine, v, jnp.zeros_like(v))
            st = dot(kh, q, NT) * (HD ** -0.5) + bias_sc[...]
            e = jnp.exp(st - jnp.max(st, axis=0, keepdims=True))
            prob = (e * (1.0 / jnp.sum(e, axis=0, keepdims=True))).astype(BF16)
            p_ref[0, 2 * p + h] = prob
            part = dot(prob, vh, TN)
            acc = part if acc is None else acc + part
        o_ref[0, :, pl.ds(p * 128, 128)] = acc.astype(BF16)
    y1 = x_ref[0] + dot(o_ref[0], wo_ref[...]) + bo_ref[...]
    y1_ref[0] = y1
    hat, _ = stats(y1)
    a2_ref[0] = (hat * g2_ref[...] + b2_ref[...]).astype(BF16)


def per_seq(a):
    return pl.BlockSpec((1, *a.shape[1:]), lambda s, *_: (s,) + (0,) * (len(a.shape) - 1))


def attn_fwd(me, bit, ff, t, w, g1, b1, bo, g2, b2):
    seqs, rows, d = t[0].shape
    length = 4 * rows
    small = (g1, b1, bo, g2, b2)
    outs = [
        struct((seqs, length, 3 * d), BF16),
        struct((seqs, 8, length, length), BF16),
        struct((seqs, length, d), BF16),
        struct((seqs, length, d), F32),
        struct((seqs, length, d), F32),
        struct((seqs, length, d), BF16),
        struct((seqs, length, d), BF16),
    ]
    weights = [struct((d, 3 * d), BF16), struct((d, d), BF16), struct((4, 8, d), F32)]
    return call(
        attn_fwd_kernel, (me, bit, ff), (*t, *w, *small), outs + weights, grid=(seqs,),
        in_specs=[per_seq(a) for a in t] + [full(a) for a in (*w, *small)],
        out_specs=[per_seq(o) for o in outs] + [full(o) for o in weights],
        scratch=[pltpu.VMEM((4, rows, d), F32), pltpu.VMEM((length, length), F32)],
        flops=2 * seqs * length * (4 * d * d + 2 * d * length), name="attention_forward")


def ff_kernel(first, me_ref, bit_ref, live_ref, *refs):
    blocks = (3, 1) if first else (2, 0)
    refs = list(refs)
    take = lambda n: [refs.pop(0) for _ in range(n)]
    weights = take(4)
    ub_ref, a2_ref = take(2)
    if first:
        cots = take(4)
    else:
        gm_ref, recv_ref = take(2)
    take(1)
    hm_ref, du_ref, g_ref, w_ref = take(4)
    if first:
        (gm_ref,) = take(1)
    wbuf, sems = take(2)
    c = pl.program_id(0)
    seqs, length, d = a2_ref.shape
    total = seqs * length
    rows = length // 4
    bit = bit_ref[0]
    copies = []
    for n, k in enumerate(blocks):
        at = (bit, 1 - bit) if k >= 2 else (0, 1)
        copies.append([
            pltpu.make_async_copy(weights[2 * n + m], wbuf.at[n, at[m]], sems.at[n, m]) for m in range(2)])
    out_copy = pltpu.make_async_copy(wbuf, w_ref, sems.at[0, 0])

    @pl.when(c == 0)
    def _():
        for group in copies:
            for cp in group:
                cp.start()
        if first:
            blk_sc, gy_sc = refs
            for s in range(seqs):
                live = live_ref[s] > 0
                for k, cot in enumerate(cots):
                    blk_sc[me_ref[0] ^ k] = jnp.where(live, cot[s].astype(F32), 0.0)
                for i in range(4):
                    gy_sc[pl.ds(i * rows, rows), :] = blk_sc[i]
                gm_ref[s] = gy_sc[...].astype(BF16)

    for n, group in enumerate(copies):
        @pl.when(c == n)
        def _():
            for cp in group:
                cp.wait()

    @pl.when(c == 1)
    def _():
        out_copy.start()

    up = wbuf[c, 0]
    dn = wbuf[c, 1]
    ub = ub_ref[jnp.where(c == 0, blocks[0], blocks[1]), 0:1]
    ubg = jnp.zeros((8, d), F32)
    for s in range(seqs):
        here = pl.ds(s * length, length)
        pre = dot(a2_ref[s], up) + ub
        dh = dot(gm_ref[s], dn, NT)
        sq = pre * pre
        t = jnp.tanh(pre * (GELU_A + (GELU_A * GELU_B) * sq))
        ht = 0.5 * t + 0.5
        slope = ht + (ht - ht * ht) * (pre * ((2 * GELU_A) + (6.0 * GELU_A * GELU_B) * sq))
        hm_ref[here, :] = (pre * ht).astype(BF16)
        du = (dh * slope).astype(BF16)
        du_ref[here, :] = du
        ubg += jnp.sum(du.astype(F32).reshape(length // 8, 8, d), axis=0)
    upg = dot(a2_ref[...].reshape(total, d), du_ref[...], TN)
    dng = dot(gm_ref[...].reshape(total, d), hm_ref[...], TN)
    ubg = jnp.sum(ubg, axis=0, keepdims=True)
    extra = jnp.where(lax.broadcasted_iota(jnp.int32, (64, d), 0) == 0, ubg, 0.0)
    if not first:
        upg += recv_ref[0, 0:d].astype(F32)
        dng += recv_ref[0, d:2 * d].astype(F32)
        extra += recv_ref[0, 2 * d:2 * d + 64].astype(F32)
    g_ref[0, 0:d, :] = upg.astype(BF16)
    g_ref[0, d:2 * d, :] = dng.astype(BF16)
    g_ref[0, 2 * d:2 * d + 64, :] = extra.astype(BF16)

    @pl.when(c == 1)
    def _():
        out_copy.wait()


def ff(first, me, bit, live, w, ub, a2, rest, after):
    seqs, length, d = a2.shape
    total = seqs * length
    anys = pl.BlockSpec(memory_space=pl.ANY)
    swap = lambda c, *_: (1 - c, 0, 0)
    g = pl.BlockSpec((1, 2 * d + 64, d), swap)
    outs = [struct((total, 2 * d), BF16)] * 2 + [struct((2, 2 * d + 64, d), BF16), struct((2, 2, d, d), BF16)]
    out_specs = [pl.BlockSpec((total, d), lambda c, *_: (0, c))] * 2 + [g, anys]
    scratch = [pltpu.VMEM((2, 2, d, d), BF16), pltpu.SemaphoreType.DMA((2, 2))]
    if first:
        rest_specs = [full(a) for a in rest]
        outs.append(struct((seqs, length, d), BF16))
        out_specs.append(full(outs[-1]))
        scratch += [pltpu.VMEM((4, length // 4, d), F32), pltpu.VMEM((length, d), F32)]
    else:
        rest_specs = [full(rest[0]), g]
    return call(
        functools.partial(ff_kernel, first), (me, bit, live), (*w, ub, a2, *rest, after), outs, grid=(2,),
        in_specs=[anys] * 4 + [full(ub), full(a2)] + rest_specs + [anys],
        out_specs=out_specs, scratch=scratch, flops=8 * total * d * d, name="feed_forward")


def attn_bwd_kernel(last, me_ref, *refs):
    refs = list(refs)
    take = lambda n: [refs.pop(0) for _ in range(n)]
    dua_ref, dub_ref, gm_ref, y1_ref, x_ref, g1_ref, g2_ref, wa_ref, wb_ref, wq_ref, wo_ref, qkv_ref, p_ref, small_in = take(14)
    if last:
        a1_ref, o_ref, dqkv_old, ga_old = take(4)
        take(4)
    take(1)
    dxs = take(4)
    if last:
        send_ref, keep_ref = take(2)
    else:
        dqkv_ref, ga_ref, small_ref = take(3)
    do_sc, full_sc, blk_sc = take(3)
    if last:
        dqkv_ref, small_ref, ga_sc, dqkv_sc = take(4)
    s = pl.program_id(0)
    _, length, d = gm_ref.shape

    @pl.when(s == 0)
    def _():
        small_ref[...] = small_in[...]

    da2 = None
    for du_ref, w_ref in ((dua_ref, wa_ref), (dub_ref, wb_ref)):
        for k in range(2):
            part = dot(du_ref[:, pl.ds(k * d, d)], w_ref[k, 0], NT)
            da2 = part if da2 is None else da2 + part
    hat, inv = stats(y1_ref[0])
    gy = gm_ref[0].astype(F32)
    dy1 = gy + norm_back(da2, hat, inv, g2_ref[...])
    full_sc[...] = dy1
    ga = dy1.astype(BF16)
    if not last:
        ga_ref[0] = ga
    sums = [jnp.sum(v, axis=0, keepdims=True) for v in (da2 * hat, da2, ga.astype(F32), gy)]
    do_sc[...] = dot(ga, wo_ref[...], NT).astype(BF16)
    lane = lax.broadcasted_iota(jnp.int32, (length, 128), 1)
    scale = HD ** -0.5
    for p in range(4):
        q = qkv_ref[0, :, pl.ds(p * 384, 128)]
        k = qkv_ref[0, :, pl.ds(p * 384 + 128, 128)]
        v = qkv_ref[0, :, pl.ds(p * 384 + 256, 128)]
        do = do_sc[:, pl.ds(p * 128, 128)]
        dq = dk = dv = None
        for h in range(2):
            mine = (lane < HD) if h == 0 else (lane >= HD)
            zero = jnp.zeros_like(q)
            qh, kh, vh, doh = (jnp.where(mine, a, zero) for a in (q, k, v, do))
            prob = p_ref[0, 2 * p + h]
            dp = dot(vh, do, NT)
            probs = prob.astype(F32)
            pd = probs * dp
            ds = (pd - probs * jnp.sum(pd, axis=0, keepdims=True)).astype(BF16)
            parts = dot(ds, kh, TN), dot(ds, qh), dot(prob, doh)
            dq, dk, dv = parts if dq is None else (dq + parts[0], dk + parts[1], dv + parts[2])
        dqkv_ref[0, :, pl.ds(p * 384, 128)] = (dq * scale).astype(BF16)
        dqkv_ref[0, :, pl.ds(p * 384 + 128, 128)] = (dk * scale).astype(BF16)
        dqkv_ref[0, :, pl.ds(p * 384 + 256, 128)] = dv.astype(BF16)

    da1 = dot(dqkv_ref[0], wq_ref[...], NT)
    hat, inv = stats(x_ref[0])
    sums += [jnp.sum(v, axis=0, keepdims=True) for v in (da1 * hat, da1)]
    full_sc[...] += norm_back(da1, hat, inv, g1_ref[...])
    spread(dxs, me_ref[0], full_sc, blk_sc)
    row = lax.broadcasted_iota(jnp.int32, (8, d), 0)
    small = jnp.zeros((8, d), F32)
    for n, v in enumerate(sums):
        small = jnp.where(row == n, v, small)
    small_ref[...] += small

    if last:
        before = dqkv_old.shape[0] * length
        for n in range(dqkv_old.shape[0]):
            dqkv_sc[pl.ds(n * length, length), :] = dqkv_old[n]
            ga_sc[pl.ds(n * length, length), :] = ga_old[n]
        dqkv_sc[pl.ds(before, length), :] = dqkv_ref[0]
        ga_sc[pl.ds(before, length), :] = ga
        total = before + length
        extra = jnp.concatenate([small_ref[...], jnp.zeros((56, d), F32)], axis=0).astype(BF16)
        for k in range(4):
            ref = send_ref if k % 2 else keep_ref
            ref[k // 2, 0:384] = dot(dqkv_sc[:, pl.ds(384 * k, 384)], a1_ref[...].reshape(total, d), TN).astype(BF16)
            ref[k // 2, 384:512] = dot(o_ref[:, :, pl.ds(128 * k, 128)].reshape(total, 128), ga_sc[...], TN).astype(BF16)
            ref[k // 2, 512:576] = extra


def attn_bwd(me, after, du, gm, y1, x, g1, g2, w, wq, wo, qkv, p, small, old=None, a1=None, o=None):
    seqs, length, d = gm.shape
    last = old is not None
    first, count = (seqs - 1, 1) if last else (0, seqs - 1)
    per = lambda a: pl.BlockSpec((1, *a.shape[1:]), lambda s, *_: (s + first,) + (0,) * (len(a.shape) - 1))
    anys = pl.BlockSpec(memory_space=pl.ANY)
    g = struct((2, 576, d), BF16)
    dx = struct((seqs, length // 4, d), BF16)
    outs = [dx] * 4
    args = [*du, gm, y1, x, g1, g2, *w, wq, wo, qkv, p, small]
    up = pl.BlockSpec((2, 1, d, d), lambda s, *_: (0, 0, 0, 0))
    in_specs = [pl.BlockSpec((length, 2 * d), lambda s, *_: (s + first, 0))] * 2 + [
        per(gm), per(y1), per(x), full(g1), full(g2), up, up, full(wq), full(wo), per(qkv), per(p), full(small)]
    out_specs = [per(a) for a in outs]
    scratch = [pltpu.VMEM((length, d), BF16), pltpu.VMEM((length, d), F32), pltpu.VMEM((4, length // 4, d), F32)]
    aliases = {}
    if last:
        dxs, dqkv, ga = old
        args += [a1, o, dqkv, ga, *dxs]
        in_specs += [full(a1), full(o), full(dqkv), full(ga), *[anys] * 4]
        aliases = {19 + k: k for k in range(4)}
        outs += [g, g]
        out_specs += [full(g), full(g)]
        scratch += [pltpu.VMEM((1, length, 3 * d), BF16), pltpu.VMEM((8, d), F32), pltpu.VMEM((seqs * length, d), BF16),
                    pltpu.VMEM((seqs * length, 3 * d), BF16)]
    else:
        extra = [struct((count, length, 3 * d), BF16), struct((count, length, d), BF16), struct((8, d), F32)]
        outs += extra
        out_specs += [per(extra[0]), per(extra[1]), full(extra[2])]
    args.append(after)
    in_specs.append(anys)
    return call(functools.partial(attn_bwd_kernel, last), (me,), args, outs, grid=(count,), in_specs=in_specs,
                out_specs=out_specs, scratch=scratch, aliases=aliases,
                flops=4 * count * length * (4 * d * d + 2 * d * length), name="attention_backward")


def spread(refs, me, full_sc, blk_sc):
    rows = blk_sc.shape[1]
    for i in range(4):
        blk_sc[i] = full_sc[pl.ds(i * rows, rows), :]
    for k, out in enumerate(refs):
        out[0] = blk_sc[me ^ k].astype(BF16)


def finish_out_kernel(me_ref, live_ref, hma_ref, hmb_ref, wa_ref, wb_ref, y1_ref, db_ref, after_ref,
                      o0, o1, o2, o3, full_sc, blk_sc):
    s = pl.program_id(0)
    d = y1_ref.shape[2]
    mlp = None
    for hm_ref, w_ref in ((hma_ref, wa_ref), (hmb_ref, wb_ref)):
        for k in range(2):
            part = dot(hm_ref[:, pl.ds(k * d, d)], w_ref[k, 0])
            mlp = part if mlp is None else mlp + part
    full_sc[...] = jnp.where(live_ref[s] > 0, y1_ref[0] + mlp + db_ref[...], 0.0)
    spread((o0, o1, o2, o3), me_ref[0], full_sc, blk_sc)


def finish_out(me, live, after, hm, w, y1, db):
    seqs, length, d = y1.shape
    outs = [struct((seqs, length // 4, d), BF16)] * 4
    down = pl.BlockSpec((2, 1, d, d), lambda s, *_: (0, 1, 0, 0))
    return call(
        finish_out_kernel, (me, live), (*hm, *w, y1, db, after), outs, grid=(seqs,),
        in_specs=[pl.BlockSpec((length, 2 * d), lambda s, *_: (s, 0))] * 2 + [
            down, down, per_seq(y1), full(db), pl.BlockSpec(memory_space=pl.ANY)],
        out_specs=[per_seq(outs[0])] * 4,
        scratch=[pltpu.VMEM((length, d), F32), pltpu.VMEM((4, length // 4, d), F32)],
        flops=2 * seqs * length * 4 * d * d, name="block_output")


def hop(value, axis, bit):
    n = lax.axis_size(axis)
    return lax.ppermute(value, axis, [(i, i ^ bit) for i in range(n)])


def split(rows, me):
    rows = rows.transpose(1, 0, 2)
    each = rows.shape[0] // 4
    return [lax.dynamic_slice_in_dim(rows, (me ^ k) * each, each) for k in range(4)]


def scatter(blocks):
    return [blocks[0]] + [hop(blocks[k], "tensor", k) for k in (1, 2, 3)]


def halves(a, side, axis=0):
    n = a.shape[axis] // 2
    return (lax.dynamic_slice_in_dim(a, side * n, n, axis), lax.dynamic_slice_in_dim(a, (1 - side) * n, n, axis))


def join(mine, other, side, axis=0):
    return jnp.where(side == 0, jnp.concatenate([mine, other], axis), jnp.concatenate([other, mine], axis))


def tie(value, *others):
    return lax.optimization_barrier((value, *others))[0]


def plus(a, b):
    return (a.astype(F32) + b.astype(F32)).astype(BF16)


class Sum:
    def __init__(self):
        self.n = lax.axis_size("dp")
        me = lax.axis_index("dp")
        self.y, self.z = me % 2, (me // 2) % 2

    def step1(self, pair):
        self.middle = middle = pair.shape[1] // 2
        self.a = pair[0, :middle]
        self.b, b_other = halves(pair[:, middle:], self.y, 1)
        self.a_got = hop(pair[1, :middle], "tensor", 2)
        self.b_got = hop(b_other, "dp", 1)
        return b_other

    def step2(self, after=()):
        a = plus(self.a, tie(self.a_got, *after))
        self.a, a_other = halves(a, self.y)
        self.a_got = hop(a_other, "dp", 1)
        self.b = plus(self.b, tie(self.b_got, *after))
        self.b_got = hop(self.b[1], "tensor", 2)
        return a_other

    def step3(self, after=()):
        a = plus(self.a, tie(self.a_got, *after))
        b = plus(self.b[0], tie(self.b_got, *after))
        self.part, other = halves(jnp.concatenate([a, b]), self.z)
        self.got = hop(other, "dp", 2)
        return other

    def step4(self, after=()):
        self.part = plus(self.part, tie(self.got, *after))
        for bit in range(2, self.n.bit_length() - 2):
            self.part = plus(self.part, hop(self.part, "dp", 1 << bit))
        self.got = hop(self.part, "dp", 1 << (self.n.bit_length() - 2))
        return self.part

    def step5(self, after=()):
        self.part = plus(self.part, tie(self.got, *after))
        self.got = hop(self.part, "dp", 2)
        return self.part

    def step6(self, after=()):
        part = join(self.part, tie(self.got, *after), self.z)
        self.part = part.reshape(2, self.middle // 2, -1)
        self.got = hop(self.part, "dp", 1)
        return self.part

    def result(self):
        return join(self.part, self.got, self.y, 1).reshape(2 * self.middle, -1)


def shards(
    tokens,
    seq_counts,
    first_frame,
    norm1_gain,
    norm1_bias,
    qkv_weight,
    out_weight,
    out_bias,
    norm2_gain,
    norm2_bias,
    up_weight,
    up_bias,
    down_weight,
    down_bias,
    out_cotangent,
):
    d = tokens.shape[2]
    seqs = tokens.shape[1] // 4
    mine = lax.axis_index("tensor").astype(jnp.int32)
    me = mine.reshape(1)
    y = lax.axis_index("dp").astype(jnp.int32) % 2
    bit = y.reshape(1)
    live = ((mine * seqs + jnp.arange(seqs, dtype=jnp.int32)) < seq_counts[0]).astype(jnp.int32)
    row = lambda a: a.reshape(1, -1)
    g1, b1, bo, g2, b2, db = map(row, (norm1_gain, norm1_bias, out_bias, norm2_gain, norm2_bias, down_bias))

    packed = pack(qkv_weight, out_weight, row(up_bias))
    far = lax.dynamic_index_in_dim(packed, y, 0, keepdims=False)
    far_a = hop(far, "tensor", 2)
    up, down = tie((up_weight, down_weight), far)
    far2_a = hop(jnp.where(y == 0, up, down), "tensor", 2)
    near = hop(packed, "tensor", 1)
    t = scatter(split(tie(tokens, far), mine))
    far_b = hop(far_a, "dp", 1)
    w1 = (packed, near, far_a, far_b, hop(far_a, "tensor", 1), hop(far_b, "tensor", 1))
    far2_b = hop(far2_a, "dp", 1)
    wa = (hop(far2_a, "tensor", 1), hop(far2_b, "tensor", 1), hop(tie(up, far_a), "tensor", 1), hop(tie(down, far_a), "tensor", 1))
    wb = (far2_a, far2_b, up_weight, down_weight)
    cot = scatter(split(tie(out_cotangent, t[2]), mine))

    qkv, p, o, x, y1, a1, a2, wq, wo, ub = attn_fwd(me, bit, first_frame, t, w1, g1, b1, bo, g2, b2)
    hma, dua, send, wa, gm = ff(True, me, bit, live, wa, ub, a2, cot, a2)
    hmb, dub, pair, wb = ff(False, me, bit, live, wb, ub, a2, (gm, hop(send, "tensor", 1)), a2)
    du, hm, w2 = (dua, dub), (hma, hmb), (wa, wb)

    mlp_sum, attn_sum = Sum(), Sum()
    ready = mlp_sum.step1(pair)
    *dx, dqkv, ga, small = attn_bwd(me, ready, du, gm, y1, x, g1, g2, w2, wq, wo, qkv, p, jnp.zeros((8, d), F32))
    ready = mlp_sum.step2((small,))
    *dx, send, keep = attn_bwd(me, ready, du, gm, y1, x, g1, g2, w2, wq, wo, qkv, p, small, (dx, dqkv, ga), a1, o)
    got = hop(send, "tensor", 1)
    ready = mlp_sum.step3((send,))
    ready = attn_sum.step1(plus(keep, tie(got, ready)))
    out = finish_out(me, live, ready, hm, w2, y1, db)
    ready = mlp_sum.step4((out[0],))
    ready = attn_sum.step2((ready,))
    dx = scatter(tie(dx, ready))
    ready = attn_sum.step3((ready,))
    ready = mlp_sum.step5((ready,))
    ready = attn_sum.step4((ready,))
    out = scatter(tie(out, dx[2], ready))
    ready = mlp_sum.step6((ready,))
    ready = attn_sum.step5((ready,))
    input_grad = place(me, tie(dx, ready)).transpose(1, 0, 2)
    ready = attn_sum.step6((ready,))
    mlp_grad = mlp_sum.result()
    attn_grad = attn_sum.result()
    block_output = place(me, out).transpose(1, 0, 2)

    mlp_grad = mlp_grad.astype(F32)
    attn_grad = attn_grad.astype(F32)
    heads = attn_grad[:384].reshape(3, 2, HD, d).transpose(1, 0, 2, 3).reshape(384, d)
    norm2_g, norm2_b, out_b, down_b, norm1_g, norm1_b = (attn_grad[512 + i] for i in range(6))
    return (
        block_output,
        input_grad,
        heads.T,
        attn_grad[384:512],
        mlp_grad[:d],
        mlp_grad[d:2 * d].T,
        mlp_grad[2 * d],
        out_b,
        down_b,
        norm1_g,
        norm1_b,
        norm2_g,
        norm2_b,
    )


def solution(mesh):
    return jax.shard_map(
        shards,
        mesh=mesh,
        in_specs=(
            P("tensor", "dp", None),
            P("dp"),
            P("dp"),
            P(),
            P(),
            P(None, "tensor"),
            P("tensor", None),
            P(),
            P(),
            P(),
            P(None, "tensor"),
            P("tensor"),
            P("tensor", None),
            P(),
            P("tensor", "dp", None),
        ),
        out_specs=(
            P("tensor", "dp", None),
            P("tensor", "dp", None),
            P(None, "tensor"),
            P("tensor", None),
            P(None, "tensor"),
            P("tensor", None),
            P("tensor"),
            P(),
            P(),
            P(),
            P(),
            P(),
            P(),
        ),
        check_vma=False,
    )
```

```python
import functools
import math

import jax
import jax.numpy as jnp
from jax import lax
from jax.experimental import pallas as pl
from jax.experimental.pallas import tpu as pltpu
from jax.sharding import PartitionSpec as P

HD = 64
FRAME_TOK = 56
BF16 = jnp.bfloat16
F32 = jnp.float32
NN = (((1,), (0,)), ((), ()))
NT = (((1,), (1,)), ((), ()))
TN = (((0,), (0,)), ((), ()))
GELU_A = 0.7978845608
GELU_B = 0.044715
VMEM_LIMIT = 40 << 20


def dot(a, b, dims=NN):
    return lax.dot_general(a, b, dims, preferred_element_type=F32)


def stats(x):
    c = x - jnp.mean(x, axis=-1, keepdims=True)
    inv = lax.rsqrt(jnp.mean(c * c, axis=-1, keepdims=True) + 1e-5)
    return c * inv, inv


def norm_back(d, hat, inv, gain):
    e = d * gain
    return inv * (
        e - jnp.mean(e, axis=-1, keepdims=True) - hat * jnp.mean(e * hat, axis=-1, keepdims=True)
    )


def full(a):
    return pl.BlockSpec(a.shape, lambda *_: (0,) * len(a.shape))


def once(shape, at=None):
    return pl.BlockSpec(shape, lambda *_: at or (0,) * len(shape), pipeline_mode=pl.Buffered(1))


def struct(shape, dtype):
    return jax.ShapeDtypeStruct(shape, dtype)


def call(kernel, scalars, args, out_shape, grid=(1,), in_specs=None, out_specs=None, scratch=(), flops=0, name=None, aliases=None, vmem=VMEM_LIMIT):
    in_specs = [full(a) for a in args] if in_specs is None else in_specs
    out_specs = [full(o) for o in out_shape] if out_specs is None else out_specs
    moved = sum(math.prod(a.shape) * a.dtype.itemsize for a in (*args, *out_shape))
    return pl.pallas_call(
        kernel,
        grid_spec=pltpu.PrefetchScalarGridSpec(
            num_scalar_prefetch=len(scalars),
            grid=grid,
            in_specs=in_specs,
            out_specs=out_specs,
            scratch_shapes=list(scratch),
        ),
        out_shape=list(out_shape),
        compiler_params=pltpu.CompilerParams(vmem_limit_bytes=vmem),
        cost_estimate=pl.CostEstimate(flops=flops, bytes_accessed=moved, transcendentals=0),
        name=name,
        input_output_aliases=aliases or {},
    )(*scalars, *args)


def pack_kernel(y_ref, z_ref, wqkv_ref, wout_ref, ub_ref, up_ref, down_ref, own_ref, far_ref):
    d = wout_ref.shape[1]
    half = d // 2
    pitch = half + 16
    ub = ub_ref[...]
    high = ub.astype(BF16).astype(F32)
    row = lax.broadcasted_iota(jnp.int32, (16, d), 0)
    ub = jnp.where(row == 0, high, jnp.where(row == 1, ub - high, 0.0)).astype(BF16)
    side = wout_ref.shape[0]
    for h in range(2):
        here = pl.ds(h * half, half)
        there = pl.ds(h * pitch, half)
        a, b, c = (wqkv_ref[here, pl.ds(128 * j, 128)].astype(F32) for j in range(3))
        low = lax.broadcasted_iota(jnp.int32, a.shape, 1) < HD
        own_ref[there, 0:128] = jnp.where(low, a, b).astype(BF16)
        own_ref[there, 128:256] = pltpu.roll(jnp.where(low, c, a), HD, 1).astype(BF16)
        own_ref[there, 256:384] = jnp.where(low, b, c).astype(BF16)
        for j in range(half // side):
            own_ref[pl.ds(h * pitch + j * side, side), 384:512] = wout_ref[:, pl.ds(h * half + 128 * j, 128)]
        own_ref[pl.ds(h * pitch + half, 16), :] = ub
    own_ref[2 * pitch:2 * pitch + d] = up_ref[...]
    own_ref[2 * pitch + d:2 * pitch + 2 * d] = down_ref[...]
    far_ref[0:2 * pitch] = own_ref[0:2 * pitch]
    at = 2 * pitch + y_ref[0] * d + z_ref[0] * half
    far_ref[2 * pitch:] = own_ref[pl.ds(pl.multiple_of(at, 16), half)]


def pack(y, z, wqkv, wout, ub, up, down):
    d = wqkv.shape[0]
    half = d // 2
    return call(pack_kernel, (y, z), (wqkv, wout, ub, up, down),
                [struct((3 * d + 32, d), BF16), struct((d + half + 32, d), BF16)], name="pack_weights")


def place_kernel(me_ref, b0, b1, b2, b3, out_ref):
    each = b0.shape[0]
    for k, b in enumerate((b0, b1, b2, b3)):
        out_ref[pl.ds((me_ref[0] ^ k) * each, each)] = b[...]


def place(me, blocks):
    each, rows, d = blocks[0].shape
    return call(place_kernel, (me,), blocks, [struct((4 * each, rows, d), BF16)], name="place")[0]


def attn_fwd_kernel(me_ref, ff_ref, t0, t1, t2, t3, w0, w1, w2, w3,
                    g1_ref, b1_ref, bo_ref, g2_ref, b2_ref,
                    qkv_ref, p_ref, o_ref, x_ref, y1_ref, a1_ref, a2_ref, wq_ref, wo_ref, ub_ref,
                    blk_sc, bias_sc, x_sc):
    s = pl.program_id(0)
    _, rows, d = t0.shape
    length = 4 * rows
    me = me_ref[0]

    @pl.when(s == 0)
    def _():
        half = d // 2
        pitch = half + 16
        for k, w in enumerate((w0, w1, w2, w3)):
            for h in range(2):
                wq_ref[pl.ds(h * half, half), pl.ds(384 * k, 384)] = w[pl.ds(h * pitch, half), 0:384]
                for j in range(half // 128):
                    wo_ref[pl.ds(128 * k, 128), pl.ds(h * half + 128 * j, 128)] = w[pl.ds(h * pitch + 128 * j, 128), 384:512]
            ub = w[half:pitch, :].astype(F32)
            ub_ref[k] = jnp.broadcast_to(ub[0:1] + ub[1:2], ub_ref.shape[1:])

    for k, t in enumerate((t0, t1, t2, t3)):
        blk_sc[me ^ k] = t[0].astype(F32)
    for i in range(4):
        x_sc[pl.ds(i * rows, rows), :] = blk_sc[i]
    x_ref[0] = x_sc[...].astype(BF16)
    hat, _ = stats(x_sc[...])
    a1 = (hat * g1_ref[...] + b1_ref[...]).astype(BF16)
    a1_ref[0] = a1
    qkv_ref[0] = dot(a1, wq_ref[...]).astype(BF16)
    start = ff_ref[me * pl.num_programs(0) + s] * FRAME_TOK
    jj = lax.broadcasted_iota(jnp.int32, (length, length), 0)
    ii = lax.broadcasted_iota(jnp.int32, (length, length), 1)
    bias_sc[...] = jnp.where((jj <= ii) & ((jj >= start) | (jj == ii)), 0.0, -1e30)
    lane = lax.broadcasted_iota(jnp.int32, (length, 128), 1)
    for p in range(4):
        q = qkv_ref[0, :, pl.ds(p * 384, 128)]
        k = qkv_ref[0, :, pl.ds(p * 384 + 128, 128)]
        v = qkv_ref[0, :, pl.ds(p * 384 + 256, 128)]
        acc = None
        for h in range(2):
            mine = (lane < HD) if h == 0 else (lane >= HD)
            kh = jnp.where(mine, k, jnp.zeros_like(k))
            vh = jnp.where(mine, v, jnp.zeros_like(v))
            st = dot(kh, q, NT) * (HD ** -0.5) + bias_sc[...]
            e = jnp.exp(st - jnp.max(st, axis=0, keepdims=True))
            prob = (e * (1.0 / jnp.sum(e, axis=0, keepdims=True))).astype(BF16)
            p_ref[0, 2 * p + h] = prob
            part = dot(prob, vh, TN)
            acc = part if acc is None else acc + part
        o_ref[0, :, pl.ds(p * 128, 128)] = acc.astype(BF16)
    y1 = x_sc[...] + dot(o_ref[0], wo_ref[...]) + bo_ref[...]
    y1_ref[0] = y1
    hat, _ = stats(y1)
    a2_ref[0] = (hat * g2_ref[...] + b2_ref[...]).astype(BF16)


def per_seq(a):
    return pl.BlockSpec((1, *a.shape[1:]), lambda s, *_: (s,) + (0,) * (len(a.shape) - 1))


def attn_fwd(me, ff, t, w, g1, b1, bo, g2, b2):
    seqs, rows, d = t[0].shape
    length = 4 * rows
    small = (g1, b1, bo, g2, b2)
    outs = [
        struct((seqs, length, 3 * d), BF16),
        struct((seqs, 8, length, length), BF16),
        struct((seqs, length, d), BF16),
        struct((seqs, length, d), BF16),
        struct((seqs, length, d), F32),
        struct((seqs, length, d), BF16),
        struct((seqs, length, d), BF16),
    ]
    weights = [struct((d, 3 * d), BF16), struct((d, d), BF16), struct((4, 8, d), F32)]
    return call(
        attn_fwd_kernel, (me, ff), (*t, *w, *small), outs + weights, grid=(seqs,),
        in_specs=[per_seq(a) for a in t] + [pl.BlockSpec((d + 32, d), lambda *_: (0, 0))] * 4 + [full(a) for a in small],
        out_specs=[per_seq(o) for o in outs] + [full(o) for o in weights],
        scratch=[pltpu.VMEM((4, rows, d), F32), pltpu.VMEM((length, length), F32), pltpu.VMEM((length, d), F32)],
        flops=2 * seqs * length * (4 * d * d + 2 * d * length), name="attention_forward", vmem=56 << 20)


def ff_kernel(me_ref, y_ref, z_ref, live_ref, w0, w1, a2_, b2_, c2_, a3_, b3_, c3_, ub_ref, a2_ref, c0, c1, c2, c3,
              hm_ref, du_ref, gm_ref, send_ref, keep_ref, w_ref, wbuf, sems, out_sems, blk_sc, row_sc):
    c = pl.program_id(0)
    seqs, length, d = a2_ref.shape
    total = seqs * length
    y, z = y_ref[0], z_ref[0]
    half = d // 2
    pitch = half + 16
    quarter = lambda k, at, side: wbuf.at[k, at, pl.ds(pl.multiple_of(side * half, half), half)]
    copies = [
        [pltpu.make_async_copy(w.at[pl.ds(2 * pitch + n * d, d)], wbuf.at[k, n], sems.at[k, n]) for n in range(2)]
        for k, w in enumerate((w0, w1))
    ] + [
        [pltpu.make_async_copy(a.at[pl.ds(2 * pitch, half)], quarter(k, y, z), sems.at[k, 0]),
         pltpu.make_async_copy(b, quarter(k, y, 1 - z), sems.at[k, 1]),
         pltpu.make_async_copy(c.at[0:half], quarter(k, 1 - y, z), sems.at[k, 2]),
         pltpu.make_async_copy(c.at[half:d], quarter(k, 1 - y, 1 - z), sems.at[k, 3])]
        for k, (a, b, c) in ((2, (a2_, b2_, c2_)), (3, (a3_, b3_, c3_)))
    ]
    out_copies = [pltpu.make_async_copy(wbuf.at[k], w_ref.at[k], out_sems.at[k]) for k in range(4)]
    order = (3, 1, 2, 0)

    @pl.when(c == 0)
    def _():
        for k in order:
            for cp in copies[k]:
                cp.start()
        rows = length // 4
        for s in range(seqs):
            live = live_ref[s] > 0
            for k, cot in enumerate((c0, c1, c2, c3)):
                blk_sc[me_ref[0] ^ k] = jnp.where(live, cot[s].astype(F32), 0.0)
            for i in range(4):
                row_sc[pl.ds(i * rows, rows), :] = blk_sc[i]
            gm_ref[s] = row_sc[...].astype(BF16)

    for n, k in enumerate(order):
        @pl.when(c == n)
        def _():
            for cp in copies[k]:
                cp.wait()
            out_copies[k].start()

    blk = jnp.where(c == 0, 3, jnp.where(c == 1, 1, jnp.where(c == 2, 2, 0)))
    up = wbuf[blk, 0]
    dn = wbuf[blk, 1]
    ub = ub_ref[blk, 0:1]
    ubg = jnp.zeros((8, d), F32)
    for s in range(seqs):
        here = pl.ds(s * length, length)
        pre = dot(a2_ref[s], up) + ub
        dh = dot(gm_ref[s], dn, NT)
        sq = pre * pre
        t = jnp.tanh(pre * (GELU_A + (GELU_A * GELU_B) * sq))
        ht = 0.5 * t + 0.5
        slope = ht + (ht - ht * ht) * (pre * ((2 * GELU_A) + (6.0 * GELU_A * GELU_B) * sq))
        hm_ref[here, :] = (pre * ht).astype(BF16)
        du = (dh * slope).astype(BF16)
        du_ref[here, :] = du
        ubg += jnp.sum(du.astype(F32).reshape(length // 8, 8, d), axis=0)
    upg = dot(a2_ref[...].reshape(total, d), du_ref[...], TN).astype(BF16)
    dng = dot(hm_ref[...], gm_ref[...].reshape(total, d), TN).astype(BF16)
    ubg = jnp.sum(ubg, axis=0, keepdims=True)
    extra = jnp.where(lax.broadcasted_iota(jnp.int32, (64, d), 0) == 0, ubg, 0.0).astype(BF16)

    @pl.when(c < 2)
    def _():
        send_ref[0, 0:d, :] = upg
        send_ref[0, d:2 * d, :] = dng
        send_ref[0, 2 * d:2 * d + 64, :] = extra

    @pl.when(c >= 2)
    def _():
        keep_ref[0, 0:d, :] = upg
        keep_ref[0, d:2 * d, :] = dng
        keep_ref[0, 2 * d:2 * d + 64, :] = extra

    @pl.when(c == 3)
    def _():
        for cp in out_copies:
            cp.wait()


def ff(me, y, z, live, w, ub, a2, cots):
    seqs, length, d = a2.shape
    total = seqs * length
    anys = pl.BlockSpec(memory_space=pl.ANY)
    column = lambda c, *_: (0, jnp.where(c == 0, 3, jnp.where(c == 1, 1, jnp.where(c == 2, 2, 0))))
    outs = [struct((total, 4 * d), BF16)] * 2 + [struct((seqs, length, d), BF16)] + [
        struct((2, 2 * d + 64, d), BF16)] * 2 + [struct((4, 2, d, d), BF16)]
    return call(
        ff_kernel, (me, y, z, live), (*w, ub, a2, *cots), outs, grid=(4,),
        in_specs=[anys] * 8 + [full(a) for a in (ub, a2, *cots)],
        out_specs=[pl.BlockSpec((total, d), column)] * 2 + [
            full(outs[2]),
            pl.BlockSpec((1, 2 * d + 64, d), lambda c, *_: (1 - jnp.minimum(c, 1), 0, 0)),
            pl.BlockSpec((1, 2 * d + 64, d), lambda c, *_: (1 - jnp.maximum(c - 2, 0), 0, 0)),
            anys],
        scratch=[pltpu.VMEM((4, 2, d, d), BF16), pltpu.SemaphoreType.DMA((4, 4)), pltpu.SemaphoreType.DMA((4,)),
                 pltpu.VMEM((4, length // 4, d), F32), pltpu.VMEM((length, d), F32)],
        flops=16 * total * d * d, name="feed_forward", vmem=44 << 20)


def attn_bwd_kernel(me_ref, du_ref, gm_ref, y1_ref, x_ref, g1_ref, g2_ref, w_ref, wq_ref, wo_ref, qkv_ref, p_ref,
                    a1_ref, o_ref, after_ref, d0, d1, d2, d3, send_ref, keep_ref,
                    do_sc, full_sc, blk_sc, small_ref, dqkv_ref, dqkv_sc, ga_sc):
    dxs = (d0, d1, d2, d3)
    s = pl.program_id(0)
    _, length, d = gm_ref.shape
    here = pl.ds(pl.multiple_of(s * length, 16), length)

    @pl.when(s == 0)
    def _():
        small_ref[...] = jnp.zeros_like(small_ref)

    da2 = None
    for k in range(4):
        part = dot(du_ref[:, pl.ds(k * d, d)], w_ref[k, 0], NT)
        da2 = part if da2 is None else da2 + part
    hat, inv = stats(y1_ref[0])
    gy = gm_ref[0].astype(F32)
    dy1 = gy + norm_back(da2, hat, inv, g2_ref[...])
    full_sc[...] = dy1
    ga = dy1.astype(BF16)
    ga_sc[here, :] = ga
    sums = [jnp.sum(v, axis=0, keepdims=True) for v in (da2 * hat, da2, ga.astype(F32), gy)]
    do_sc[...] = dot(ga, wo_ref[...], NT).astype(BF16)
    lane = lax.broadcasted_iota(jnp.int32, (length, 128), 1)
    scale = HD ** -0.5
    for p in range(4):
        q = qkv_ref[0, :, pl.ds(p * 384, 128)]
        k = qkv_ref[0, :, pl.ds(p * 384 + 128, 128)]
        v = qkv_ref[0, :, pl.ds(p * 384 + 256, 128)]
        do = do_sc[:, pl.ds(p * 128, 128)]
        dq = dk = dv = None
        for h in range(2):
            mine = (lane < HD) if h == 0 else (lane >= HD)
            zero = jnp.zeros_like(q)
            qh, kh, vh, doh = (jnp.where(mine, a, zero) for a in (q, k, v, do))
            prob = p_ref[0, 2 * p + h]
            dp = dot(vh, do, NT)
            probs = prob.astype(F32)
            pd = probs * dp
            ds = (pd - probs * jnp.sum(pd, axis=0, keepdims=True)).astype(BF16)
            parts = dot(ds, kh, TN), dot(ds, qh), dot(prob, doh)
            dq, dk, dv = parts if dq is None else (dq + parts[0], dk + parts[1], dv + parts[2])
        dqkv_ref[0, :, pl.ds(p * 384, 128)] = (dq * scale).astype(BF16)
        dqkv_ref[0, :, pl.ds(p * 384 + 128, 128)] = (dk * scale).astype(BF16)
        dqkv_ref[0, :, pl.ds(p * 384 + 256, 128)] = dv.astype(BF16)

    da1 = dot(dqkv_ref[0], wq_ref[...], NT)
    hat, inv = stats(x_ref[0].astype(F32))
    sums += [jnp.sum(v, axis=0, keepdims=True) for v in (da1 * hat, da1)]
    full_sc[...] += norm_back(da1, hat, inv, g1_ref[...])
    spread(dxs, me_ref[0], full_sc, blk_sc)
    row = lax.broadcasted_iota(jnp.int32, (8, d), 0)
    small = jnp.zeros((8, d), F32)
    for n, v in enumerate(sums):
        small = jnp.where(row == n, v, small)
    small_ref[...] += small


    dqkv_sc[here, :] = dqkv_ref[0]

    @pl.when(s == pl.num_programs(0) - 1)
    def _():
        total = dqkv_sc.shape[0]
        extra = jnp.concatenate([small_ref[...], jnp.zeros((56, d), F32)], axis=0).astype(BF16)
        for k in range(4):
            ref = send_ref if k % 2 else keep_ref
            ref[k // 2, 0:384] = dot(dqkv_sc[:, pl.ds(384 * k, 384)], a1_ref[...].reshape(total, d), TN).astype(BF16)
            ref[k // 2, 384:512] = dot(o_ref[:, :, pl.ds(128 * k, 128)].reshape(total, 128), ga_sc[...], TN).astype(BF16)
            ref[k // 2, 512:576] = extra


def attn_bwd(me, after, du, gm, y1, x, g1, g2, w, wq, wo, qkv, p, a1, o):
    seqs, length, d = gm.shape
    total = seqs * length
    anys = pl.BlockSpec(memory_space=pl.ANY)
    outs = [struct((seqs, length // 4, d), BF16)] * 4 + [struct((2, 576, d), BF16)] * 2
    args = [du, gm, y1, x, g1, g2, w, wq, wo, qkv, p, a1, o, after]
    in_specs = [pl.BlockSpec((length, 4 * d), lambda s, *_: (s, 0)), per_seq(gm), per_seq(y1), per_seq(x), full(g1), full(g2),
                once((4, 1, d, d)), once(wq.shape), once(wo.shape), per_seq(qkv), per_seq(p), once(a1.shape), once(o.shape), anys]
    scratch = [pltpu.VMEM((length, d), BF16), pltpu.VMEM((length, d), F32), pltpu.VMEM((4, length // 4, d), F32),
               pltpu.VMEM((8, d), F32), pltpu.VMEM((1, length, 3 * d), BF16), pltpu.VMEM((total, 3 * d), BF16),
               pltpu.VMEM((total, d), BF16)]
    return call(attn_bwd_kernel, (me,), args, outs, grid=(seqs,), in_specs=in_specs,
                out_specs=[per_seq(a) for a in outs[:4]] + [once(a.shape) for a in outs[4:]], scratch=scratch,
                flops=6 * total * (4 * d * d + 2 * d * length), name="attention_backward", vmem=40 << 20)


def spread(refs, me, full_sc, blk_sc):
    rows = blk_sc.shape[1]
    for i in range(4):
        blk_sc[i] = full_sc[pl.ds(i * rows, rows), :]
    for k, out in enumerate(refs):
        out[0] = blk_sc[me ^ k].astype(BF16)


def finish_out_kernel(me_ref, live_ref, hm_ref, w_ref, y1_ref, db_ref, after_ref, o0, o1, o2, o3, full_sc, blk_sc):
    s = pl.program_id(0)
    d = y1_ref.shape[2]
    mlp = None
    for k in range(4):
        part = dot(hm_ref[:, pl.ds(k * d, d)], w_ref[k, 0])
        mlp = part if mlp is None else mlp + part
    full_sc[...] = jnp.where(live_ref[s] > 0, y1_ref[0] + mlp + db_ref[...], 0.0)
    spread((o0, o1, o2, o3), me_ref[0], full_sc, blk_sc)


def finish_out(me, live, after, hm, w, y1, db):
    seqs, length, d = y1.shape
    outs = [struct((seqs, length // 4, d), BF16)] * 4
    return call(
        finish_out_kernel, (me, live), (hm, w, y1, db, after), outs, grid=(seqs,),
        in_specs=[pl.BlockSpec((length, 4 * d), lambda s, *_: (s, 0)),
                  pl.BlockSpec((4, 1, d, d), lambda s, *_: (0, 1, 0, 0)), per_seq(y1), full(db),
                  pl.BlockSpec(memory_space=pl.ANY)],
        out_specs=[per_seq(outs[0])] * 4,
        scratch=[pltpu.VMEM((length, d), F32), pltpu.VMEM((4, length // 4, d), F32)],
        flops=2 * seqs * length * 4 * d * d, name="block_output", vmem=56 << 20)


def hop(value, axis, bit):
    n = lax.axis_size(axis)
    return lax.ppermute(value, axis, [(i, i ^ bit) for i in range(n)])


def split(rows, me):
    rows = rows.transpose(1, 0, 2)
    each = rows.shape[0] // 4
    return [lax.dynamic_slice_in_dim(rows, (me ^ k) * each, each) for k in range(4)]


def scatter(blocks):
    return [blocks[0]] + [hop(blocks[k], "tensor", k) for k in (1, 2, 3)]


def halves(a, side, axis=0):
    n = a.shape[axis] // 2
    return (lax.dynamic_slice_in_dim(a, side * n, n, axis), lax.dynamic_slice_in_dim(a, (1 - side) * n, n, axis))


def join(mine, other, side, axis=0):
    return jnp.where(side == 0, jnp.concatenate([mine, other], axis), jnp.concatenate([other, mine], axis))


def tie(value, *others):
    return lax.optimization_barrier((value, *others))[0]


def plus(a, b):
    return (a.astype(F32) + b.astype(F32)).astype(BF16)


def wait(after, *groups):
    sizes = [len(g) for g in groups]
    flat = lax.optimization_barrier((*[a for g in groups for a in g], *after))
    out = []
    for n in sizes:
        out.append(list(flat[:n]))
        flat = flat[n:]
    return out


class Sum:
    def __init__(self, one, two):
        self.n = lax.axis_size("dp")
        me = lax.axis_index("dp")
        self.one, self.two = one, two
        self.y, self.z = (me // one) % 2, (me // two) % 2

    def step1(self, pair):
        self.middle = middle = pair.shape[1] // 2
        self.a = pair[0, :middle]
        a_other = pair[1, :middle]
        self.b, b_other = halves(pair[:, middle:], self.y, 1)
        self.got = [hop(a_other, "tensor", 2), hop(b_other, "dp", self.one)]
        return [a_other, b_other]

    def step2(self):
        self.a, a_other = halves(plus(self.a, self.got[0]), self.y)
        b = plus(self.b, self.got[1])
        self.b, b_other = b[0], b[1]
        self.got = [hop(a_other, "dp", self.one), hop(b_other, "tensor", 2)]
        return [a_other, b_other]

    def step3(self):
        both = jnp.concatenate([plus(self.a, self.got[0]), plus(self.b, self.got[1])])
        self.part, other = halves(both, self.z)
        self.got = [hop(other, "dp", self.two)]
        return [other]

    def step4(self):
        self.part = plus(self.part, self.got[0])
        top = self.n.bit_length() - 2
        for bit in range(2, top):
            self.part = plus(self.part, hop(self.part, "dp", 1 << bit))
        self.got = [hop(self.part, "dp", 1 << top)]
        return [self.part]

    def step5(self):
        part = plus(self.part, self.got[0])
        n = part.shape[0] // 2
        self.h1, self.h2 = part[:n], part[n:]
        self.got = [hop(self.h1, "dp", self.two), hop(self.h2, "dp", self.one)]
        return [self.h1, self.h2]

    def step6(self):
        pick = lambda mine, other, side: jnp.where(side == 0, jnp.stack([mine, other]), jnp.stack([other, mine]))
        self.h1 = pick(self.h1, self.got[0], self.z)
        self.h2 = pick(self.h2, self.got[1], self.y)
        self.got = [hop(self.h1, "dp", self.one), hop(self.h2, "dp", self.two)]
        return [self.h1, self.h2]

    def result(self):
        pick = lambda mine, other, side, axis: jnp.where(
            side == 0, jnp.stack([mine, other], axis), jnp.stack([other, mine], axis))
        h1 = pick(self.h1, self.got[0], self.y, 1)
        h2 = pick(self.h2, self.got[1], self.z, 0)
        return jnp.concatenate([h1, h2], axis=2).reshape(2 * self.middle, -1)


def shards(
    tokens,
    seq_counts,
    first_frame,
    norm1_gain,
    norm1_bias,
    qkv_weight,
    out_weight,
    out_bias,
    norm2_gain,
    norm2_bias,
    up_weight,
    up_bias,
    down_weight,
    down_bias,
    out_cotangent,
):
    d = tokens.shape[2]
    seqs = tokens.shape[1] // 4
    mine = lax.axis_index("tensor").astype(jnp.int32)
    me = mine.reshape(1)
    y = lax.axis_index("dp").astype(jnp.int32) % 2
    bit = y.reshape(1)
    live = ((mine * seqs + jnp.arange(seqs, dtype=jnp.int32)) < seq_counts[0]).astype(jnp.int32)
    row = lambda a: a.reshape(1, -1)
    g1, b1, bo, g2, b2, db = map(row, (norm1_gain, norm1_bias, out_bias, norm2_gain, norm2_bias, down_bias))

    z = (lax.axis_index("dp").astype(jnp.int32) // 2) % 2
    zbit = z.reshape(1)
    own, far = pack(bit, zbit, qkv_weight, out_weight, row(up_bias), up_weight, down_weight)
    far_a = hop(far, "tensor", 2)
    near = hop(own, "tensor", 1)
    t = split(tie(tokens, near), mine)
    t = [t[0]] + [hop(t[k], "tensor", k) for k in (1, 2, 3)]
    far_2 = far_a[d + 32:]
    far_b = hop(far_2, "dp", 2)
    diag_a, diag_b = hop(tie(far_a, t[1]), "tensor", 1), hop(far_b, "tensor", 1)
    far_c = hop(tie(jnp.concatenate([far_2, far_b]), diag_a, t[1], t[2], t[3]), "dp", 1)
    w1 = (own, near, far_a, diag_a)
    cot = scatter(split(tie(out_cotangent, t[1], t[2]), mine))

    qkv, p, o, x, y1, a1, a2, wq, wo, ub = attn_fwd(me, first_frame, t, w1, g1, b1, bo, g2, b2)
    w2 = (own, near, far_a, far_b, far_c, diag_a, diag_b, hop(tie(far_c, a2, *cot), "tensor", 1))
    hm, du, gm, send, keep, w2 = ff(me, bit, zbit, live, w2, ub, a2, cot)

    m, a = Sum(1, 2), Sum(2, 1)
    got = hop(send, "tensor", 1)
    out = finish_out(me, live, a2, hm, w2, y1, db)
    ((got,),) = wait(out, [got])
    sent = m.step1(plus(keep, got))
    out = scatter(tie(out, *sent))
    *dx, send, keep = attn_bwd(me, tie(*sent), du, gm, y1, x, g1, g2, w2, wq, wo, qkv, p, a1, o)
    m.got, out = wait([send], m.got, out)
    sent = m.step2()
    got = hop(tie(send, *sent), "tensor", 1)
    ((got,),) = wait(sent, [got])
    sent = a.step1(plus(keep, got))
    block_output = place(me, tie(out, *sent)).transpose(1, 0, 2)
    (m.got,) = wait([block_output], m.got)
    sent = m.step3()
    (a.got,) = wait(sent, a.got)
    sent = a.step2()
    dx = scatter(tie(dx, *sent))
    (m.got,) = wait(sent, m.got)
    sent = m.step4()
    (a.got,) = wait(sent, a.got)
    sent = a.step3()
    a.got, dx = wait(sent, a.got, dx)
    sent = a.step4()
    input_grad = place(me, tie(dx, *sent)).transpose(1, 0, 2)
    (m.got,) = wait([input_grad], m.got)
    sent = m.step5()
    (a.got,) = wait(sent, a.got)
    sent = a.step5()
    (m.got,) = wait(sent, m.got)
    sent = m.step6()
    (a.got,) = wait(sent, a.got)
    sent = a.step6()
    (m.got,) = wait(sent, m.got)
    mlp_grad = m.result()
    (a.got,) = wait([mlp_grad], a.got)
    attn_grads = a.result()

    mlp_grad = mlp_grad.astype(F32)
    attn_grads = attn_grads.astype(F32)
    heads = attn_grads[:384].reshape(3, 2, HD, d).transpose(1, 0, 2, 3).reshape(384, d)
    norm2_g, norm2_b, out_b, down_b, norm1_g, norm1_b = (attn_grads[512 + i] for i in range(6))
    return (
        block_output,
        input_grad,
        heads.T,
        attn_grads[384:512],
        mlp_grad[:d],
        mlp_grad[d:2 * d],
        mlp_grad[2 * d],
        out_b,
        down_b,
        norm1_g,
        norm1_b,
        norm2_g,
        norm2_b,
    )


def solution(mesh):
    return jax.shard_map(
        shards,
        mesh=mesh,
        in_specs=(
            P("tensor", "dp", None),
            P("dp"),
            P("dp"),
            P(),
            P(),
            P(None, "tensor"),
            P("tensor", None),
            P(),
            P(),
            P(),
            P(None, "tensor"),
            P("tensor"),
            P("tensor", None),
            P(),
            P("tensor", "dp", None),
        ),
        out_specs=(
            P("tensor", "dp", None),
            P("tensor", "dp", None),
            P(None, "tensor"),
            P("tensor", None),
            P(None, "tensor"),
            P("tensor", None),
            P("tensor"),
            P(),
            P(),
            P(),
            P(),
            P(),
            P(),
        ),
        check_vma=False,
    )
```

```python
import functools
import math

import jax
import jax.numpy as jnp
from jax import lax
from jax.experimental import pallas as pl
from jax.experimental.pallas import tpu as pltpu
from jax.sharding import PartitionSpec as P

HD = 64
FRAME_TOK = 56
BF16 = jnp.bfloat16
F32 = jnp.float32
NN = (((1,), (0,)), ((), ()))
NT = (((1,), (1,)), ((), ()))
TN = (((0,), (0,)), ((), ()))
GELU_A = 0.7978845608
GELU_B = 0.044715
VMEM_LIMIT = 40 << 20


def dot(a, b, dims=NN):
    return lax.dot_general(a, b, dims, preferred_element_type=F32)


def stats(x):
    c = x - jnp.mean(x, axis=-1, keepdims=True)
    inv = lax.rsqrt(jnp.mean(c * c, axis=-1, keepdims=True) + 1e-5)
    return c * inv, inv


def norm_back(d, hat, inv, gain):
    e = d * gain
    return inv * (
        e - jnp.mean(e, axis=-1, keepdims=True) - hat * jnp.mean(e * hat, axis=-1, keepdims=True)
    )


def full(a):
    return pl.BlockSpec(a.shape, lambda *_: (0,) * len(a.shape))


def once(shape, at=None):
    return pl.BlockSpec(shape, lambda *_: at or (0,) * len(shape), pipeline_mode=pl.Buffered(1))


def struct(shape, dtype):
    return jax.ShapeDtypeStruct(shape, dtype)


def call(kernel, scalars, args, out_shape, grid=(1,), in_specs=None, out_specs=None, scratch=(), flops=0, name=None, aliases=None, vmem=VMEM_LIMIT):
    in_specs = [full(a) for a in args] if in_specs is None else in_specs
    out_specs = [full(o) for o in out_shape] if out_specs is None else out_specs
    moved = sum(math.prod(a.shape) * a.dtype.itemsize for a in (*args, *out_shape))
    return pl.pallas_call(
        kernel,
        grid_spec=pltpu.PrefetchScalarGridSpec(
            num_scalar_prefetch=len(scalars),
            grid=grid,
            in_specs=in_specs,
            out_specs=out_specs,
            scratch_shapes=list(scratch),
        ),
        out_shape=list(out_shape),
        compiler_params=pltpu.CompilerParams(vmem_limit_bytes=vmem),
        cost_estimate=pl.CostEstimate(flops=flops, bytes_accessed=moved, transcendentals=0),
        name=name,
        input_output_aliases=aliases or {},
    )(*scalars, *args)


def pack_kernel(y_ref, z_ref, wqkv_ref, wout_ref, ub_ref, up_ref, down_ref, own_ref, far_ref):
    d = wout_ref.shape[1]
    half = d // 2
    pitch = half + 16
    ub = ub_ref[...]
    high = ub.astype(BF16).astype(F32)
    row = lax.broadcasted_iota(jnp.int32, (16, d), 0)
    ub = jnp.where(row == 0, high, jnp.where(row == 1, ub - high, 0.0)).astype(BF16)
    side = wout_ref.shape[0]
    for h in range(2):
        here = pl.ds(h * half, half)
        there = pl.ds(h * pitch, half)
        a, b, c = (wqkv_ref[here, pl.ds(128 * j, 128)].astype(F32) for j in range(3))
        low = lax.broadcasted_iota(jnp.int32, a.shape, 1) < HD
        own_ref[there, 0:128] = jnp.where(low, a, b).astype(BF16)
        own_ref[there, 128:256] = pltpu.roll(jnp.where(low, c, a), HD, 1).astype(BF16)
        own_ref[there, 256:384] = jnp.where(low, b, c).astype(BF16)
        for j in range(half // side):
            own_ref[pl.ds(h * pitch + j * side, side), 384:512] = wout_ref[:, pl.ds(h * half + 128 * j, 128)]
        own_ref[pl.ds(h * pitch + half, 16), :] = ub
    own_ref[2 * pitch:2 * pitch + d] = up_ref[...]
    own_ref[2 * pitch + d:2 * pitch + 2 * d] = down_ref[...]
    far_ref[0:2 * pitch] = own_ref[0:2 * pitch]
    at = 2 * pitch + y_ref[0] * d + z_ref[0] * half
    far_ref[2 * pitch:] = own_ref[pl.ds(pl.multiple_of(at, 16), half)]


def pack(y, z, wqkv, wout, ub, up, down):
    d = wqkv.shape[0]
    half = d // 2
    return call(pack_kernel, (y, z), (wqkv, wout, ub, up, down),
                [struct((3 * d + 32, d), BF16), struct((d + half + 32, d), BF16)], name="pack_weights", vmem=56 << 20)


def place_kernel(me_ref, b0, b1, b2, b3, out_ref):
    each = b0.shape[0]
    for k, b in enumerate((b0, b1, b2, b3)):
        out_ref[pl.ds((me_ref[0] ^ k) * each, each)] = b[...]


def far_specs(a):
    return [pl.BlockSpec((a.shape[0] // 2, *a.shape[1:]), lambda *_, n=n: (n, 0, 0)) for n in range(2)]


def far_seq_specs(a):
    return [pl.BlockSpec((1, *a.shape[1:]), lambda s, *_, n=n: (n * (a.shape[0] // 2) + s, 0, 0)) for n in range(2)]


def place(me, blocks):
    each, rows, d = blocks[0].shape
    return call(place_kernel, (me,), blocks, [struct((4 * each, rows, d), BF16)],
                in_specs=[full(blocks[0]), full(blocks[1])] + far_specs(blocks[2]), name="place")[0]


def attn_fwd_kernel(me_ref, ff_ref, t0, t1, t2, t3, w0, w1, w2, w3,
                    g1_ref, b1_ref, bo_ref, g2_ref, b2_ref,
                    qkv_ref, p_ref, o_ref, x_ref, y1_ref, a1_ref, a2_ref, wq_ref, wo_ref, ub_ref,
                    blk_sc, bias_sc, x_sc):
    s = pl.program_id(0)
    _, rows, d = t0.shape
    length = 4 * rows
    me = me_ref[0]

    @pl.when(s == 0)
    def _():
        half = d // 2
        pitch = half + 16
        for k, w in enumerate((w0, w1, w2, w3)):
            for h in range(2):
                wq_ref[pl.ds(h * half, half), pl.ds(384 * k, 384)] = w[pl.ds(h * pitch, half), 0:384]
                for j in range(half // 128):
                    wo_ref[pl.ds(128 * k, 128), pl.ds(h * half + 128 * j, 128)] = w[pl.ds(h * pitch + 128 * j, 128), 384:512]
            ub = w[half:pitch, :].astype(F32)
            ub_ref[k] = jnp.broadcast_to(ub[0:1] + ub[1:2], ub_ref.shape[1:])

    for k, t in enumerate((t0, t1, t2, t3)):
        blk_sc[me ^ k] = t[0].astype(F32)
    for i in range(4):
        x_sc[pl.ds(i * rows, rows), :] = blk_sc[i]
    x_ref[0] = x_sc[...].astype(BF16)
    hat, _ = stats(x_sc[...])
    a1 = (hat * g1_ref[...] + b1_ref[...]).astype(BF16)
    a1_ref[0] = a1
    qkv_ref[0] = dot(a1, wq_ref[...]).astype(BF16)
    start = ff_ref[me * pl.num_programs(0) + s] * FRAME_TOK
    jj = lax.broadcasted_iota(jnp.int32, (length, length), 0)
    ii = lax.broadcasted_iota(jnp.int32, (length, length), 1)
    bias_sc[...] = jnp.where((jj <= ii) & ((jj >= start) | (jj == ii)), 0.0, -1e30)
    lane = lax.broadcasted_iota(jnp.int32, (length, 128), 1)
    for p in range(4):
        q = qkv_ref[0, :, pl.ds(p * 384, 128)]
        k = qkv_ref[0, :, pl.ds(p * 384 + 128, 128)]
        v = qkv_ref[0, :, pl.ds(p * 384 + 256, 128)]
        acc = None
        for h in range(2):
            mine = (lane < HD) if h == 0 else (lane >= HD)
            kh = jnp.where(mine, k, jnp.zeros_like(k))
            vh = jnp.where(mine, v, jnp.zeros_like(v))
            st = dot(kh, q, NT) * (HD ** -0.5) + bias_sc[...]
            e = jnp.exp(st - jnp.max(st, axis=0, keepdims=True))
            prob = (e * (1.0 / jnp.sum(e, axis=0, keepdims=True))).astype(BF16)
            p_ref[0, 2 * p + h] = prob
            part = dot(prob, vh, TN)
            acc = part if acc is None else acc + part
        o_ref[0, :, pl.ds(p * 128, 128)] = acc.astype(BF16)
    y1 = x_sc[...] + dot(o_ref[0], wo_ref[...]) + bo_ref[...]
    y1_ref[0] = y1
    hat, _ = stats(y1)
    a2_ref[0] = (hat * g2_ref[...] + b2_ref[...]).astype(BF16)


def per_seq(a):
    return pl.BlockSpec((1, *a.shape[1:]), lambda s, *_: (s,) + (0,) * (len(a.shape) - 1))


def attn_fwd(me, ff, t, w, g1, b1, bo, g2, b2):
    seqs, rows, d = t[0].shape
    length = 4 * rows
    small = (g1, b1, bo, g2, b2)
    outs = [
        struct((seqs, length, 3 * d), BF16),
        struct((seqs, 8, length, length), BF16),
        struct((seqs, length, d), BF16),
        struct((seqs, length, d), BF16),
        struct((seqs, length, d), F32),
        struct((seqs, length, d), BF16),
        struct((seqs, length, d), BF16),
    ]
    weights = [struct((d, 3 * d), BF16), struct((d, d), BF16), struct((4, 8, d), F32)]
    return call(
        attn_fwd_kernel, (me, ff), (*t, *w, *small), outs + weights, grid=(seqs,),
        in_specs=[per_seq(a) for a in t[:2]] + far_seq_specs(t[2]) + [pl.BlockSpec((d + 32, d), lambda *_: (0, 0))] * 4 + [full(a) for a in small],
        out_specs=[per_seq(o) for o in outs] + [full(o) for o in weights],
        scratch=[pltpu.VMEM((4, rows, d), F32), pltpu.VMEM((length, length), F32), pltpu.VMEM((length, d), F32)],
        flops=2 * seqs * length * (4 * d * d + 2 * d * length), name="attention_forward", vmem=56 << 20)


def ff_kernel(me_ref, y_ref, z_ref, count_ref, w0, w1, a2_, b2_, c2_, d2_, a3_, b3_, c3_, d3_, ub_ref, a2_ref, c0, c1, c2, c3,
              hm_ref, du_ref, gm_ref, send_ref, keep_ref, w_ref, wbuf, sems, out_sems, blk_sc, row_sc):
    c = pl.program_id(0)
    seqs, length, d = a2_ref.shape
    total = seqs * length
    y, z = y_ref[0], z_ref[0]
    half = d // 2
    pitch = half + 16
    quarter = lambda k, at, side: wbuf.at[k, at, pl.ds(pl.multiple_of(side * half, half), half)]
    copies = [
        [pltpu.make_async_copy(w.at[pl.ds(2 * pitch + n * d, d)], wbuf.at[k, n], sems.at[k, n]) for n in range(2)]
        for k, w in enumerate((w0, w1))
    ] + [
        [pltpu.make_async_copy(a.at[pl.ds(2 * pitch, half)], quarter(k, y, z), sems.at[k, 0]),
         pltpu.make_async_copy(b, quarter(k, y, 1 - z), sems.at[k, 1]),
         pltpu.make_async_copy(c, quarter(k, 1 - y, z), sems.at[k, 2]),
         pltpu.make_async_copy(e, quarter(k, 1 - y, 1 - z), sems.at[k, 3])]
        for k, (a, b, c, e) in ((2, (a2_, b2_, c2_, d2_)), (3, (a3_, b3_, c3_, d3_)))
    ]
    out_copies = [pltpu.make_async_copy(wbuf.at[k], w_ref.at[k], out_sems.at[k]) for k in range(4)]
    order = (3, 1, 2, 0)

    @pl.when(c == 0)
    def _():
        for k in order:
            for cp in copies[k]:
                cp.start()
        rows = length // 4
        for s in range(seqs):
            live = me_ref[0] * seqs + s < count_ref[0]
            for k, cot in enumerate((c0, c1, c2, c3)):
                blk_sc[me_ref[0] ^ k] = jnp.where(live, cot[s].astype(F32), 0.0)
            for i in range(4):
                row_sc[pl.ds(i * rows, rows), :] = blk_sc[i]
            gm_ref[s] = row_sc[...].astype(BF16)

    for n, k in enumerate(order):
        @pl.when(c == n)
        def _():
            for cp in copies[k]:
                cp.wait()
            out_copies[k].start()

    blk = jnp.where(c == 0, 3, jnp.where(c == 1, 1, jnp.where(c == 2, 2, 0)))
    up = wbuf[blk, 0]
    dn = wbuf[blk, 1]
    ub = ub_ref[blk, 0:1]
    ubg = jnp.zeros((8, d), F32)
    for s in range(seqs):
        here = pl.ds(s * length, length)
        pre = dot(a2_ref[s], up) + ub
        dh = dot(gm_ref[s], dn, NT)
        sq = pre * pre
        t = jnp.tanh(pre * (GELU_A + (GELU_A * GELU_B) * sq))
        ht = 0.5 * t + 0.5
        slope = ht + (ht - ht * ht) * (pre * ((2 * GELU_A) + (6.0 * GELU_A * GELU_B) * sq))
        hm_ref[here, :] = (pre * ht).astype(BF16)
        du = (dh * slope).astype(BF16)
        du_ref[here, :] = du
        ubg += jnp.sum(du.astype(F32).reshape(length // 8, 8, d), axis=0)
    upg = dot(a2_ref[...].reshape(total, d), du_ref[...], TN).astype(BF16)
    dng = dot(hm_ref[...], gm_ref[...].reshape(total, d), TN).astype(BF16)
    ubg = jnp.sum(ubg, axis=0, keepdims=True)
    extra = jnp.where(lax.broadcasted_iota(jnp.int32, (64, d), 0) == 0, ubg, 0.0).astype(BF16)

    @pl.when(c < 2)
    def _():
        send_ref[0, 0:d, :] = upg
        send_ref[0, d:2 * d, :] = dng
        send_ref[0, 2 * d:2 * d + 64, :] = extra

    @pl.when(c >= 2)
    def _():
        keep_ref[0, 0:d, :] = upg
        keep_ref[0, d:2 * d, :] = dng
        keep_ref[0, 2 * d:2 * d + 64, :] = extra

    @pl.when(c == 3)
    def _():
        for cp in out_copies:
            cp.wait()


def ff(me, y, z, count, w, ub, a2, cots):
    seqs, length, d = a2.shape
    total = seqs * length
    anys = pl.BlockSpec(memory_space=pl.ANY)
    column = lambda c, *_: (0, jnp.where(c == 0, 3, jnp.where(c == 1, 1, jnp.where(c == 2, 2, 0))))
    outs = [struct((total, 4 * d), BF16)] * 2 + [struct((seqs, length, d), BF16)] + [
        struct((2, 2 * d + 64, d), BF16)] * 2 + [struct((4, 2, d, d), BF16)]
    return call(
        ff_kernel, (me, y, z, count), (*w, ub, a2, *cots), outs, grid=(4,),
        in_specs=[anys] * 10 + [full(a) for a in (ub, a2, *cots[:2])] + far_specs(cots[2]),
        out_specs=[pl.BlockSpec((total, d), column)] * 2 + [
            full(outs[2]),
            pl.BlockSpec((1, 2 * d + 64, d), lambda c, *_: (1 - jnp.minimum(c, 1), 0, 0)),
            pl.BlockSpec((1, 2 * d + 64, d), lambda c, *_: (1 - jnp.maximum(c - 2, 0), 0, 0)),
            anys],
        scratch=[pltpu.VMEM((4, 2, d, d), BF16), pltpu.SemaphoreType.DMA((4, 4)), pltpu.SemaphoreType.DMA((4,)),
                 pltpu.VMEM((4, length // 4, d), F32), pltpu.VMEM((length, d), F32)],
        flops=16 * total * d * d, name="feed_forward", vmem=56 << 20)


def attn_bwd_kernel(me_ref, du_ref, gm_ref, y1_ref, x_ref, g1_ref, g2_ref, w_ref, wq_ref, wo_ref, qkv_ref, p_ref,
                    a1_ref, o_ref, after_ref, d0, d1, d2, send_ref, keep_ref,
                    do_sc, full_sc, blk_sc, small_ref, dqkv_ref, dqkv_sc, ga_sc):
    dxs = (d0, d1, d2)
    s = pl.program_id(0)
    _, length, d = gm_ref.shape
    here = pl.ds(pl.multiple_of(s * length, 16), length)

    @pl.when(s == 0)
    def _():
        small_ref[...] = jnp.zeros_like(small_ref)

    da2 = None
    for k in range(4):
        part = dot(du_ref[:, pl.ds(k * d, d)], w_ref[k, 0], NT)
        da2 = part if da2 is None else da2 + part
    hat, inv = stats(y1_ref[0])
    gy = gm_ref[0].astype(F32)
    dy1 = gy + norm_back(da2, hat, inv, g2_ref[...])
    full_sc[...] = dy1
    ga = dy1.astype(BF16)
    ga_sc[here, :] = ga
    sums = [jnp.sum(v, axis=0, keepdims=True) for v in (da2 * hat, da2, ga.astype(F32), gy)]
    do_sc[...] = dot(ga, wo_ref[...], NT).astype(BF16)
    lane = lax.broadcasted_iota(jnp.int32, (length, 128), 1)
    scale = HD ** -0.5
    for p in range(4):
        q = qkv_ref[0, :, pl.ds(p * 384, 128)]
        k = qkv_ref[0, :, pl.ds(p * 384 + 128, 128)]
        v = qkv_ref[0, :, pl.ds(p * 384 + 256, 128)]
        do = do_sc[:, pl.ds(p * 128, 128)]
        dq = dk = dv = None
        for h in range(2):
            mine = (lane < HD) if h == 0 else (lane >= HD)
            zero = jnp.zeros_like(q)
            qh, kh, vh, doh = (jnp.where(mine, a, zero) for a in (q, k, v, do))
            prob = p_ref[0, 2 * p + h]
            dp = dot(vh, do, NT)
            probs = prob.astype(F32)
            pd = probs * dp
            ds = (pd - probs * jnp.sum(pd, axis=0, keepdims=True)).astype(BF16)
            parts = dot(ds, kh, TN), dot(ds, qh), dot(prob, doh)
            dq, dk, dv = parts if dq is None else (dq + parts[0], dk + parts[1], dv + parts[2])
        dqkv_ref[0, :, pl.ds(p * 384, 128)] = (dq * scale).astype(BF16)
        dqkv_ref[0, :, pl.ds(p * 384 + 128, 128)] = (dk * scale).astype(BF16)
        dqkv_ref[0, :, pl.ds(p * 384 + 256, 128)] = dv.astype(BF16)

    da1 = dot(dqkv_ref[0], wq_ref[...], NT)
    hat, inv = stats(x_ref[0].astype(F32))
    sums += [jnp.sum(v, axis=0, keepdims=True) for v in (da1 * hat, da1)]
    full_sc[...] += norm_back(da1, hat, inv, g1_ref[...])
    spread(dxs, me_ref[0], full_sc, blk_sc)
    row = lax.broadcasted_iota(jnp.int32, (8, d), 0)
    small = jnp.zeros((8, d), F32)
    for n, v in enumerate(sums):
        small = jnp.where(row == n, v, small)
    small_ref[...] += small


    dqkv_sc[here, :] = dqkv_ref[0]

    @pl.when(s == pl.num_programs(0) - 1)
    def _():
        total = dqkv_sc.shape[0]
        extra = jnp.concatenate([small_ref[...], jnp.zeros((56, d), F32)], axis=0).astype(BF16)
        for k in range(4):
            ref = send_ref if k % 2 else keep_ref
            ref[k // 2, 0:384] = dot(dqkv_sc[:, pl.ds(384 * k, 384)], a1_ref[...].reshape(total, d), TN).astype(BF16)
            ref[k // 2, 384:512] = dot(o_ref[:, :, pl.ds(128 * k, 128)].reshape(total, 128), ga_sc[...], TN).astype(BF16)
            ref[k // 2, 512:576] = extra


def attn_bwd(me, after, du, gm, y1, x, g1, g2, w, wq, wo, qkv, p, a1, o):
    seqs, length, d = gm.shape
    total = seqs * length
    anys = pl.BlockSpec(memory_space=pl.ANY)
    outs, out_specs = spread_outs(seqs, length // 4, d)
    grads = [struct((2, 576, d), BF16)] * 2
    args = [du, gm, y1, x, g1, g2, w, wq, wo, qkv, p, a1, o, after]
    in_specs = [pl.BlockSpec((length, 4 * d), lambda s, *_: (s, 0)), per_seq(gm), per_seq(y1), per_seq(x), full(g1), full(g2),
                once((4, 1, d, d)), once(wq.shape), once(wo.shape), per_seq(qkv), per_seq(p), once(a1.shape), once(o.shape), anys]
    scratch = [pltpu.VMEM((length, d), BF16), pltpu.VMEM((length, d), F32), pltpu.VMEM((4, length // 4, d), F32),
               pltpu.VMEM((8, d), F32), pltpu.VMEM((1, length, 3 * d), BF16), pltpu.VMEM((total, 3 * d), BF16),
               pltpu.VMEM((total, d), BF16)]
    return call(attn_bwd_kernel, (me,), args, outs + grads, grid=(seqs,), in_specs=in_specs,
                out_specs=out_specs + [once(a.shape) for a in grads], scratch=scratch,
                flops=6 * total * (4 * d * d + 2 * d * length), name="attention_backward", vmem=40 << 20)


def spread(refs, me, full_sc, blk_sc):
    rows = blk_sc.shape[1]
    for i in range(4):
        blk_sc[i] = full_sc[pl.ds(i * rows, rows), :]
    own, near, far = refs
    s = pl.program_id(0)
    each = far.shape[0] // 2
    own[0] = blk_sc[me].astype(BF16)
    near[0] = blk_sc[me ^ 1].astype(BF16)
    far[s] = blk_sc[me ^ 2].astype(BF16)
    far[each + s] = blk_sc[me ^ 3].astype(BF16)


def spread_outs(seqs, rows, d):
    one = struct((seqs, rows, d), BF16)
    far = struct((2 * seqs, rows, d), BF16)
    return [one, one, far], [per_seq(one), per_seq(one), once(far.shape)]


def finish_out_kernel(me_ref, count_ref, hm_ref, w_ref, y1_ref, db_ref, after_ref, o0, o1, o2, full_sc, blk_sc):
    s = pl.program_id(0)
    d = y1_ref.shape[2]
    mlp = None
    for k in range(4):
        part = dot(hm_ref[:, pl.ds(k * d, d)], w_ref[k, 0])
        mlp = part if mlp is None else mlp + part
    full_sc[...] = jnp.where(me_ref[0] * pl.num_programs(0) + s < count_ref[0], y1_ref[0] + mlp + db_ref[...], 0.0)
    spread((o0, o1, o2), me_ref[0], full_sc, blk_sc)


def finish_out(me, count, after, hm, w, y1, db):
    seqs, length, d = y1.shape
    outs, out_specs = spread_outs(seqs, length // 4, d)
    return call(
        finish_out_kernel, (me, count), (hm, w, y1, db, after), outs, grid=(seqs,),
        in_specs=[pl.BlockSpec((length, 4 * d), lambda s, *_: (s, 0)),
                  pl.BlockSpec((4, 1, d, d), lambda s, *_: (0, 1, 0, 0)), per_seq(y1), full(db),
                  pl.BlockSpec(memory_space=pl.ANY)],
        out_specs=out_specs,
        scratch=[pltpu.VMEM((length, d), F32), pltpu.VMEM((4, length // 4, d), F32)],
        flops=2 * seqs * length * 4 * d * d, name="block_output", vmem=56 << 20)


def hop(value, axis, bit):
    n = lax.axis_size(axis)
    return lax.ppermute(value, axis, [(i, i ^ bit) for i in range(n)])


def split(rows, me):
    rows = rows.transpose(1, 0, 2)
    each = rows.shape[0] // 4
    own, near, *far = (lax.dynamic_slice_in_dim(rows, (me ^ k) * each, each) for k in range(4))
    return [own, near, jnp.concatenate(far)]


def exchange(own, near, far):
    far = hop(far, "tensor", 2)
    return [own, hop(near, "tensor", 1), far, far]


def forward(blocks, *after):
    return [*blocks[:3], hop(tie(blocks[3], *after), "tensor", 1)]


def halves(a, side, axis=0):
    n = a.shape[axis] // 2
    return (lax.dynamic_slice_in_dim(a, side * n, n, axis), lax.dynamic_slice_in_dim(a, (1 - side) * n, n, axis))


def join(mine, other, side, axis=0):
    return jnp.where(side == 0, jnp.concatenate([mine, other], axis), jnp.concatenate([other, mine], axis))


def tie(value, *others):
    return lax.optimization_barrier((value, *others))[0]


def plus(a, b):
    return (a.astype(F32) + b.astype(F32)).astype(BF16)


def wait(after, *groups):
    sizes = [len(g) for g in groups]
    flat = lax.optimization_barrier((*[a for g in groups for a in g], *after))
    out = []
    for n in sizes:
        out.append(list(flat[:n]))
        flat = flat[n:]
    return out


class Sum:
    def __init__(self, one, two):
        self.n = lax.axis_size("dp")
        me = lax.axis_index("dp")
        self.one, self.two = one, two
        self.y, self.z = (me // one) % 2, (me // two) % 2

    def step1(self, pair):
        self.middle = middle = pair.shape[1] // 2
        self.a = pair[0, :middle]
        a_other = pair[1, :middle]
        self.b, b_other = halves(pair[:, middle:], self.y, 1)
        self.got = [hop(a_other, "tensor", 2), hop(b_other, "dp", self.one)]
        return [a_other, b_other]

    def step2(self):
        self.a, a_other = halves(plus(self.a, self.got[0]), self.y)
        b = plus(self.b, self.got[1])
        self.b, b_other = b[0], b[1]
        self.got = [hop(a_other, "dp", self.one), hop(b_other, "tensor", 2)]
        return [a_other, b_other]

    def step3(self):
        both = jnp.concatenate([plus(self.a, self.got[0]), plus(self.b, self.got[1])])
        self.part, other = halves(both, self.z)
        self.got = [hop(other, "dp", self.two)]
        return [other]

    def step4(self):
        self.part = plus(self.part, self.got[0])
        top = self.n.bit_length() - 2
        for bit in range(2, top):
            self.part = plus(self.part, hop(self.part, "dp", 1 << bit))
        self.got = [hop(self.part, "dp", 1 << top)]
        return [self.part]

    def step5(self):
        part = plus(self.part, self.got[0])
        n = part.shape[0] // 2
        self.h1, self.h2 = part[:n], part[n:]
        self.got = [hop(self.h1, "dp", self.two), hop(self.h2, "dp", self.one)]
        return [self.h1, self.h2]

    def step6(self):
        pick = lambda mine, other, side: jnp.where(side == 0, jnp.stack([mine, other]), jnp.stack([other, mine]))
        self.h1 = pick(self.h1, self.got[0], self.z)
        self.h2 = pick(self.h2, self.got[1], self.y)
        self.got = [hop(self.h1, "dp", self.one), hop(self.h2, "dp", self.two)]
        return [self.h1, self.h2]

    def result(self):
        pick = lambda mine, other, side, axis: jnp.where(
            side == 0, jnp.stack([mine, other], axis), jnp.stack([other, mine], axis))
        h1 = pick(self.h1, self.got[0], self.y, 1)
        h2 = pick(self.h2, self.got[1], self.z, 0)
        return jnp.concatenate([h1, h2], axis=2).reshape(2 * self.middle, -1)


def shards(
    tokens,
    seq_counts,
    first_frame,
    norm1_gain,
    norm1_bias,
    qkv_weight,
    out_weight,
    out_bias,
    norm2_gain,
    norm2_bias,
    up_weight,
    up_bias,
    down_weight,
    down_bias,
    out_cotangent,
):
    d = tokens.shape[2]
    seqs = tokens.shape[1] // 4
    mine = lax.axis_index("tensor").astype(jnp.int32)
    me = mine.reshape(1)
    y = lax.axis_index("dp").astype(jnp.int32) % 2
    bit = y.reshape(1)
    row = lambda a: a.reshape(1, -1)
    g1, b1, bo, g2, b2, db = map(row, (norm1_gain, norm1_bias, out_bias, norm2_gain, norm2_bias, down_bias))

    z = (lax.axis_index("dp").astype(jnp.int32) // 2) % 2
    zbit = z.reshape(1)
    own, far = pack(bit, zbit, qkv_weight, out_weight, row(up_bias), up_weight, down_weight)
    far_a = hop(far, "tensor", 2)
    near = hop(own, "tensor", 1)
    t = split(tie(tokens, near), mine)
    t_far, t_near = hop(t[2], "tensor", 2), hop(t[1], "tensor", 1)
    cot = split(tie(out_cotangent, t[2]), mine)
    cot_near = hop(cot[1], "tensor", 1)
    far_a = tie(far_a, t_far, t_near, cot[2], cot_near)
    t = [t[0], t_near, t_far, hop(tie(t_far, far_a), "tensor", 1)]
    diag_a = hop(far_a, "tensor", 1)
    far_2 = far_a[d + 32:]
    far_2 = [far_2, hop(far_2, "dp", 2), hop(far_2, "dp", 1), hop(far_2, "dp", 3)]
    w1 = (own, near, far_a, diag_a)
    cot_far = hop(tie(cot[2], t_far), "tensor", 2)

    qkv, p, o, x, y1, a1, a2, wq, wo, ub = attn_fwd(me, first_frame, t, w1, g1, b1, bo, g2, b2)
    near_2 = tie(far_2[1:], a2)
    cot = forward([cot[0], cot_near, cot_far, cot_far], a2)
    w2 = (own, near, far_a, *far_2[1:], diag_a, *(hop(b, "tensor", 1) for b in near_2))
    hm, du, gm, send, keep, w2 = ff(me, bit, zbit, seq_counts, w2, ub, a2, cot)

    m, a = Sum(1, 2), Sum(2, 1)
    got = hop(send, "tensor", 1)
    out = finish_out(me, seq_counts, a2, hm, w2, y1, db)
    ((got,),) = wait(out, [got])
    sent = m.step1(plus(keep, got))
    out = exchange(*tie(out, *sent))
    *dx, send, keep = attn_bwd(me, tie(*sent), du, gm, y1, x, g1, g2, w2, wq, wo, qkv, p, a1, o)
    m.got, out = wait([send], m.got, out[:3])
    out = forward([*out, out[2]])
    sent = m.step2()
    got = hop(tie(send, *sent), "tensor", 1)
    ((got,),) = wait(sent, [got])
    sent = a.step1(plus(keep, got))
    block_output = place(me, tie(out, *sent)).transpose(1, 0, 2)
    (m.got,) = wait([block_output], m.got)
    sent = m.step3()
    (a.got,) = wait(sent, a.got)
    sent = a.step2()
    dx = exchange(*tie(dx, *sent))
    (m.got,) = wait(sent, m.got)
    sent = m.step4()
    (a.got,) = wait(sent, a.got)
    sent = a.step3()
    (m.got,) = wait(sent, m.got)
    sent = m.step5()
    a.got, dx = wait(sent, a.got, dx[:3])
    sent = a.step4()
    dx = forward([*dx, dx[2]], *sent)
    (m.got,) = wait(sent, m.got)
    sent = m.step6()
    input_grad = place(me, tie(dx, *sent)).transpose(1, 0, 2)
    (a.got,) = wait([input_grad], a.got)
    sent = a.step5()
    (m.got,) = wait(sent, m.got)
    mlp_grad = m.result()
    (a.got,) = wait([mlp_grad], a.got)
    a.step6()
    attn_grads = a.result()

    mlp_grad = mlp_grad.astype(F32)
    attn_grads = attn_grads.astype(F32)
    heads = attn_grads[:384].reshape(3, 2, HD, d).transpose(1, 0, 2, 3).reshape(384, d)
    norm2_g, norm2_b, out_b, down_b, norm1_g, norm1_b = (attn_grads[512 + i] for i in range(6))
    return (
        block_output,
        input_grad,
        heads.T,
        attn_grads[384:512],
        mlp_grad[:d],
        mlp_grad[d:2 * d],
        mlp_grad[2 * d],
        out_b,
        down_b,
        norm1_g,
        norm1_b,
        norm2_g,
        norm2_b,
    )


def solution(mesh):
    return jax.shard_map(
        shards,
        mesh=mesh,
        in_specs=(
            P("tensor", "dp", None),
            P("dp"),
            P("dp"),
            P(),
            P(),
            P(None, "tensor"),
            P("tensor", None),
            P(),
            P(),
            P(),
            P(None, "tensor"),
            P("tensor"),
            P("tensor", None),
            P(),
            P("tensor", "dp", None),
        ),
        out_specs=(
            P("tensor", "dp", None),
            P("tensor", "dp", None),
            P(None, "tensor"),
            P("tensor", None),
            P(None, "tensor"),
            P("tensor", None),
            P("tensor"),
            P(),
            P(),
            P(),
            P(),
            P(),
            P(),
        ),
        check_vma=False,
    )
```

```python
import functools
import math

import jax
import jax.numpy as jnp
from jax import lax
from jax.experimental import pallas as pl
from jax.experimental.pallas import tpu as pltpu
from jax.sharding import PartitionSpec as P

HD = 64
FRAME_TOK = 56
BF16 = jnp.bfloat16
F32 = jnp.float32
NN = (((1,), (0,)), ((), ()))
NT = (((1,), (1,)), ((), ()))
TN = (((0,), (0,)), ((), ()))
GELU_A = 0.7978845608
GELU_B = 0.044715
VMEM_LIMIT = 40 << 20


def dot(a, b, dims=NN):
    return lax.dot_general(a, b, dims, preferred_element_type=F32)


def stats(x):
    c = x - jnp.mean(x, axis=-1, keepdims=True)
    inv = lax.rsqrt(jnp.mean(c * c, axis=-1, keepdims=True) + 1e-5)
    return c * inv, inv


def norm_back(d, hat, inv, gain):
    e = d * gain
    return inv * (
        e - jnp.mean(e, axis=-1, keepdims=True) - hat * jnp.mean(e * hat, axis=-1, keepdims=True)
    )


def full(a):
    return pl.BlockSpec(a.shape, lambda *_: (0,) * len(a.shape))


def once(shape, at=None):
    return pl.BlockSpec(shape, lambda *_: at or (0,) * len(shape), pipeline_mode=pl.Buffered(1))


def struct(shape, dtype):
    return jax.ShapeDtypeStruct(shape, dtype)


def call(kernel, scalars, args, out_shape, grid=(1,), in_specs=None, out_specs=None, scratch=(), flops=0, name=None, aliases=None, vmem=VMEM_LIMIT):
    in_specs = [full(a) for a in args] if in_specs is None else in_specs
    out_specs = [full(o) for o in out_shape] if out_specs is None else out_specs
    moved = sum(math.prod(a.shape) * a.dtype.itemsize for a in (*args, *out_shape))
    return pl.pallas_call(
        kernel,
        grid_spec=pltpu.PrefetchScalarGridSpec(
            num_scalar_prefetch=len(scalars),
            grid=grid,
            in_specs=in_specs,
            out_specs=out_specs,
            scratch_shapes=list(scratch),
        ),
        out_shape=list(out_shape),
        compiler_params=pltpu.CompilerParams(vmem_limit_bytes=vmem),
        cost_estimate=pl.CostEstimate(flops=flops, bytes_accessed=moved, transcendentals=0),
        name=name,
        input_output_aliases=aliases or {},
    )(*scalars, *args)


def pack_kernel(y_ref, z_ref, wqkv_ref, wout_ref, ub_ref, up_ref, down_ref, own_ref, far_ref):
    d = wout_ref.shape[1]
    half = d // 2
    pitch = half + 16
    ub = ub_ref[...]
    high = ub.astype(BF16).astype(F32)
    row = lax.broadcasted_iota(jnp.int32, (16, d), 0)
    ub = jnp.where(row == 0, high, jnp.where(row == 1, ub - high, 0.0)).astype(BF16)
    side = wout_ref.shape[0]
    for h in range(2):
        here = pl.ds(h * half, half)
        there = pl.ds(h * pitch, half)
        a, b, c = (wqkv_ref[here, pl.ds(128 * j, 128)].astype(F32) for j in range(3))
        low = lax.broadcasted_iota(jnp.int32, a.shape, 1) < HD
        own_ref[there, 0:128] = jnp.where(low, a, b).astype(BF16)
        own_ref[there, 128:256] = pltpu.roll(jnp.where(low, c, a), HD, 1).astype(BF16)
        own_ref[there, 256:384] = jnp.where(low, b, c).astype(BF16)
        for j in range(half // side):
            own_ref[pl.ds(h * pitch + j * side, side), 384:512] = wout_ref[:, pl.ds(h * half + 128 * j, 128)]
        own_ref[pl.ds(h * pitch + half, 16), :] = ub
    own_ref[2 * pitch:2 * pitch + d] = up_ref[...]
    own_ref[2 * pitch + d:2 * pitch + 2 * d] = down_ref[...]
    far_ref[0:2 * pitch] = own_ref[0:2 * pitch]
    at = 2 * pitch + y_ref[0] * d + z_ref[0] * half
    far_ref[2 * pitch:] = own_ref[pl.ds(pl.multiple_of(at, 16), half)]


def pack(y, z, wqkv, wout, ub, up, down):
    d = wqkv.shape[0]
    half = d // 2
    return call(pack_kernel, (y, z), (wqkv, wout, ub, up, down),
                [struct((3 * d + 32, d), BF16), struct((d + half + 32, d), BF16)], name="pack_weights", vmem=56 << 20)


def place_kernel(me_ref, b0, b1, b2, b3, out_ref):
    each = b0.shape[0]
    for k, b in enumerate((b0, b1, b2, b3)):
        out_ref[pl.ds((me_ref[0] ^ k) * each, each)] = b[...]


def far_specs(a):
    return [pl.BlockSpec((a.shape[0] // 2, *a.shape[1:]), lambda *_, n=n: (n, 0, 0)) for n in range(2)]


def far_seq_specs(a):
    return [pl.BlockSpec((1, *a.shape[1:]), lambda s, *_, n=n: (n * (a.shape[0] // 2) + s, 0, 0)) for n in range(2)]


def place(me, blocks):
    each, rows, d = blocks[0].shape
    return call(place_kernel, (me,), blocks, [struct((4 * each, rows, d), BF16)],
                in_specs=[full(blocks[0]), full(blocks[1])] + far_specs(blocks[2]), name="place")[0]


def attn_fwd_kernel(me_ref, ff_ref, t0, t1, t2, t3, w0, w1, w2, w3,
                    g1_ref, b1_ref, bo_ref, g2_ref, b2_ref,
                    qkv_ref, p_ref, o_ref, x_ref, y1_ref, a1_ref, a2_ref, wq_ref, wo_ref, ub_ref,
                    blk_sc, bias_sc, x_sc):
    s = pl.program_id(0)
    _, rows, d = t0.shape
    length = 4 * rows
    me = me_ref[0]

    @pl.when(s == 0)
    def _():
        half = d // 2
        pitch = half + 16
        for k, w in enumerate((w0, w1, w2, w3)):
            for h in range(2):
                wq_ref[pl.ds(h * half, half), pl.ds(384 * k, 384)] = w[pl.ds(h * pitch, half), 0:384]
                for j in range(half // 128):
                    wo_ref[pl.ds(128 * k, 128), pl.ds(h * half + 128 * j, 128)] = w[pl.ds(h * pitch + 128 * j, 128), 384:512]
            ub = w[half:pitch, :].astype(F32)
            ub_ref[k] = jnp.broadcast_to(ub[0:1] + ub[1:2], ub_ref.shape[1:])

    for k, t in enumerate((t0, t1, t2, t3)):
        blk_sc[me ^ k] = t[0].astype(F32)
    for i in range(4):
        x_sc[pl.ds(i * rows, rows), :] = blk_sc[i]
    x_ref[0] = x_sc[...].astype(BF16)
    hat, _ = stats(x_sc[...])
    a1 = (hat * g1_ref[...] + b1_ref[...]).astype(BF16)
    a1_ref[0] = a1
    qkv_ref[0] = dot(a1, wq_ref[...]).astype(BF16)
    start = ff_ref[me * pl.num_programs(0) + s] * FRAME_TOK
    jj = lax.broadcasted_iota(jnp.int32, (length, length), 0)
    ii = lax.broadcasted_iota(jnp.int32, (length, length), 1)
    bias_sc[...] = jnp.where((jj <= ii) & ((jj >= start) | (jj == ii)), 0.0, -1e30)
    lane = lax.broadcasted_iota(jnp.int32, (length, 128), 1)
    for p in range(4):
        q = qkv_ref[0, :, pl.ds(p * 384, 128)]
        k = qkv_ref[0, :, pl.ds(p * 384 + 128, 128)]
        v = qkv_ref[0, :, pl.ds(p * 384 + 256, 128)]
        acc = None
        for h in range(2):
            mine = (lane < HD) if h == 0 else (lane >= HD)
            kh = jnp.where(mine, k, jnp.zeros_like(k))
            vh = jnp.where(mine, v, jnp.zeros_like(v))
            st = dot(kh, q, NT) * (HD ** -0.5) + bias_sc[...]
            e = jnp.exp(st - jnp.max(st, axis=0, keepdims=True))
            prob = (e * (1.0 / jnp.sum(e, axis=0, keepdims=True))).astype(BF16)
            p_ref[0, 2 * p + h] = prob
            part = dot(prob, vh, TN)
            acc = part if acc is None else acc + part
        o_ref[0, :, pl.ds(p * 128, 128)] = acc.astype(BF16)
    y1 = x_sc[...] + dot(o_ref[0], wo_ref[...]) + bo_ref[...]
    y1_ref[0] = y1
    hat, _ = stats(y1)
    a2_ref[0] = (hat * g2_ref[...] + b2_ref[...]).astype(BF16)


def per_seq(a):
    return pl.BlockSpec((1, *a.shape[1:]), lambda s, *_: (s,) + (0,) * (len(a.shape) - 1))


def attn_fwd(me, ff, t, w, g1, b1, bo, g2, b2):
    seqs, rows, d = t[0].shape
    length = 4 * rows
    small = (g1, b1, bo, g2, b2)
    outs = [
        struct((seqs, length, 3 * d), BF16),
        struct((seqs, 8, length, length), BF16),
        struct((seqs, length, d), BF16),
        struct((seqs, length, d), BF16),
        struct((seqs, length, d), F32),
        struct((seqs, length, d), BF16),
        struct((seqs, length, d), BF16),
    ]
    weights = [struct((d, 3 * d), BF16), struct((d, d), BF16), struct((4, 8, d), F32)]
    return call(
        attn_fwd_kernel, (me, ff), (*t, *w, *small), outs + weights, grid=(seqs,),
        in_specs=[per_seq(a) for a in t[:2]] + far_seq_specs(t[2]) + [pl.BlockSpec((d + 32, d), lambda *_: (0, 0))] * 4 + [full(a) for a in small],
        out_specs=[per_seq(o) for o in outs] + [full(o) for o in weights],
        scratch=[pltpu.VMEM((4, rows, d), F32), pltpu.VMEM((length, length), F32), pltpu.VMEM((length, d), F32)],
        flops=2 * seqs * length * (4 * d * d + 2 * d * length), name="attention_forward", vmem=56 << 20)


def ff_kernel(me_ref, y_ref, z_ref, count_ref, w0, w1, a2_, b2_, c2_, d2_, a3_, b3_, c3_, d3_, ub_ref, a2_ref, c0, c1, c2, c3,
              hm_ref, du_ref, gm_ref, send_ref, keep_ref, w_ref, wbuf, sems, out_sems, blk_sc, row_sc):
    c = pl.program_id(0)
    seqs, length, d = a2_ref.shape
    total = seqs * length
    y, z = y_ref[0], z_ref[0]
    half = d // 2
    pitch = half + 16
    quarter = lambda k, at, side: wbuf.at[k, at, pl.ds(pl.multiple_of(side * half, half), half)]
    copies = [
        [pltpu.make_async_copy(w.at[pl.ds(2 * pitch + n * d, d)], wbuf.at[k, n], sems.at[k, n]) for n in range(2)]
        for k, w in enumerate((w0, w1))
    ] + [
        [pltpu.make_async_copy(a.at[pl.ds(2 * pitch, half)], quarter(k, y, z), sems.at[k, 0]),
         pltpu.make_async_copy(b, quarter(k, y, 1 - z), sems.at[k, 1]),
         pltpu.make_async_copy(c, quarter(k, 1 - y, z), sems.at[k, 2]),
         pltpu.make_async_copy(e, quarter(k, 1 - y, 1 - z), sems.at[k, 3])]
        for k, (a, b, c, e) in ((2, (a2_, b2_, c2_, d2_)), (3, (a3_, b3_, c3_, d3_)))
    ]
    out_copies = [pltpu.make_async_copy(wbuf.at[k], w_ref.at[k], out_sems.at[k]) for k in range(4)]
    order = (3, 1, 2, 0)

    @pl.when(c == 0)
    def _():
        for k in order:
            for cp in copies[k]:
                cp.start()
        rows = length // 4
        for s in range(seqs):
            live = me_ref[0] * seqs + s < count_ref[0]
            for k, cot in enumerate((c0, c1, c2, c3)):
                blk_sc[me_ref[0] ^ k] = jnp.where(live, cot[s].astype(F32), 0.0)
            for i in range(4):
                row_sc[pl.ds(i * rows, rows), :] = blk_sc[i]
            gm_ref[s] = row_sc[...].astype(BF16)

    for n, k in enumerate(order):
        @pl.when(c == n)
        def _():
            for cp in copies[k]:
                cp.wait()
            out_copies[k].start()

    blk = jnp.where(c == 0, 3, jnp.where(c == 1, 1, jnp.where(c == 2, 2, 0)))
    up = wbuf[blk, 0]
    dn = wbuf[blk, 1]
    ub = ub_ref[blk, 0:1]
    ubg = jnp.zeros((8, d), F32)
    for s in range(seqs):
        here = pl.ds(s * length, length)
        pre = dot(a2_ref[s], up) + ub
        dh = dot(gm_ref[s], dn, NT)
        sq = pre * pre
        t = jnp.tanh(pre * (GELU_A + (GELU_A * GELU_B) * sq))
        ht = 0.5 * t + 0.5
        slope = ht + (ht - ht * ht) * (pre * ((2 * GELU_A) + (6.0 * GELU_A * GELU_B) * sq))
        hm_ref[here, :] = (pre * ht).astype(BF16)
        du = (dh * slope).astype(BF16)
        du_ref[here, :] = du
        ubg += jnp.sum(du.astype(F32).reshape(length // 8, 8, d), axis=0)
    upg = dot(a2_ref[...].reshape(total, d), du_ref[...], TN).astype(BF16)
    dng = dot(hm_ref[...], gm_ref[...].reshape(total, d), TN).astype(BF16)
    ubg = jnp.sum(ubg, axis=0, keepdims=True)
    extra = jnp.where(lax.broadcasted_iota(jnp.int32, (64, d), 0) == 0, ubg, 0.0).astype(BF16)

    @pl.when(c < 2)
    def _():
        send_ref[0, 0:d, :] = upg
        send_ref[0, d:2 * d, :] = dng
        send_ref[0, 2 * d:2 * d + 64, :] = extra

    @pl.when(c >= 2)
    def _():
        keep_ref[0, 0:d, :] = upg
        keep_ref[0, d:2 * d, :] = dng
        keep_ref[0, 2 * d:2 * d + 64, :] = extra

    @pl.when(c == 3)
    def _():
        for cp in out_copies:
            cp.wait()


def ff(me, y, z, count, w, ub, a2, cots):
    seqs, length, d = a2.shape
    total = seqs * length
    anys = pl.BlockSpec(memory_space=pl.ANY)
    column = lambda c, *_: (0, jnp.where(c == 0, 3, jnp.where(c == 1, 1, jnp.where(c == 2, 2, 0))))
    outs = [struct((total, 4 * d), BF16)] * 2 + [struct((seqs, length, d), BF16)] + [
        struct((2, 2 * d + 64, d), BF16)] * 2 + [struct((4, 2, d, d), BF16)]
    return call(
        ff_kernel, (me, y, z, count), (*w, ub, a2, *cots), outs, grid=(4,),
        in_specs=[anys] * 10 + [full(a) for a in (ub, a2, *cots[:2])] + far_specs(cots[2]),
        out_specs=[pl.BlockSpec((total, d), column)] * 2 + [
            full(outs[2]),
            pl.BlockSpec((1, 2 * d + 64, d), lambda c, *_: (1 - jnp.minimum(c, 1), 0, 0)),
            pl.BlockSpec((1, 2 * d + 64, d), lambda c, *_: (1 - jnp.maximum(c - 2, 0), 0, 0)),
            anys],
        scratch=[pltpu.VMEM((4, 2, d, d), BF16), pltpu.SemaphoreType.DMA((4, 4)), pltpu.SemaphoreType.DMA((4,)),
                 pltpu.VMEM((4, length // 4, d), F32), pltpu.VMEM((length, d), F32)],
        flops=16 * total * d * d, name="feed_forward", vmem=56 << 20)


def attn_bwd_kernel(me_ref, du_ref, gm_ref, y1_ref, x_ref, g1_ref, g2_ref, w_ref, wq_ref, wo_ref, qkv_ref, p_ref,
                    a1_ref, o_ref, after_ref, d0, d1, d2, send_ref, keep_ref,
                    do_sc, full_sc, blk_sc, small_ref, dqkv_ref, dqkv_sc, ga_sc):
    dxs = (d0, d1, d2)
    s = pl.program_id(0)
    _, length, d = gm_ref.shape
    here = pl.ds(pl.multiple_of(s * length, 16), length)

    @pl.when(s == 0)
    def _():
        small_ref[...] = jnp.zeros_like(small_ref)

    da2 = None
    for k in range(4):
        part = dot(du_ref[:, pl.ds(k * d, d)], w_ref[k, 0], NT)
        da2 = part if da2 is None else da2 + part
    hat, inv = stats(y1_ref[0])
    gy = gm_ref[0].astype(F32)
    dy1 = gy + norm_back(da2, hat, inv, g2_ref[...])
    full_sc[...] = dy1
    ga = dy1.astype(BF16)
    ga_sc[here, :] = ga
    sums = [jnp.sum(v, axis=0, keepdims=True) for v in (da2 * hat, da2, ga.astype(F32), gy)]
    do_sc[...] = dot(ga, wo_ref[...], NT).astype(BF16)
    lane = lax.broadcasted_iota(jnp.int32, (length, 128), 1)
    scale = HD ** -0.5
    cut = min(256, length)
    for p in range(4):
        q = qkv_ref[0, :, pl.ds(p * 384, 128)]
        k = qkv_ref[0, :, pl.ds(p * 384 + 128, 128)]
        v = qkv_ref[0, :, pl.ds(p * 384 + 256, 128)]
        do = do_sc[:, pl.ds(p * 128, 128)]
        for h in range(2):
            mine = (lane < HD) if h == 0 else (lane >= HD)
            zero = jnp.zeros_like(q)
            qh, kh, vh, doh = (jnp.where(mine, a, zero) for a in (q, k, v, do))
            prob = p_ref[0, 2 * p + h]
            dp = dot(vh, do, NT)
            probs = prob.astype(F32)
            pd = probs * dp
            ds = (pd - probs * jnp.sum(pd, axis=0, keepdims=True)).astype(BF16)
            pq = dot(ds[:cut, :cut], kh[:cut], TN), dot(ds[:, cut:], kh, TN)
            pk = dot(ds[:cut], qh), dot(ds[cut:, cut:], qh[cut:])
            pv = dot(prob[:cut], doh), dot(prob[cut:, cut:], doh[cut:])
            parts = (pq, pk, pv)
            total = parts if h == 0 else [[b + c for b, c in zip(*pair)] for pair in zip(total, parts)]
        for n, (kind, factor) in enumerate(zip(total, (scale, scale, 1.0))):
            for rows, value in zip((pl.ds(0, cut), pl.ds(cut, length - cut)), kind):
                dqkv_ref[0, rows, pl.ds(p * 384 + 128 * n, 128)] = (value * factor).astype(BF16)

    da1 = dot(dqkv_ref[0], wq_ref[...], NT)
    hat, inv = stats(x_ref[0].astype(F32))
    sums += [jnp.sum(v, axis=0, keepdims=True) for v in (da1 * hat, da1)]
    full_sc[...] += norm_back(da1, hat, inv, g1_ref[...])
    spread(dxs, me_ref[0], full_sc, blk_sc)
    row = lax.broadcasted_iota(jnp.int32, (8, d), 0)
    small = jnp.zeros((8, d), F32)
    for n, v in enumerate(sums):
        small = jnp.where(row == n, v, small)
    small_ref[...] += small


    dqkv_sc[here, :] = dqkv_ref[0]

    @pl.when(s == pl.num_programs(0) - 1)
    def _():
        total = dqkv_sc.shape[0]
        extra = jnp.concatenate([small_ref[...], jnp.zeros((56, d), F32)], axis=0).astype(BF16)
        for k in range(4):
            ref = send_ref if k % 2 else keep_ref
            ref[k // 2, 0:384] = dot(dqkv_sc[:, pl.ds(384 * k, 384)], a1_ref[...].reshape(total, d), TN).astype(BF16)
            ref[k // 2, 384:512] = dot(o_ref[:, :, pl.ds(128 * k, 128)].reshape(total, 128), ga_sc[...], TN).astype(BF16)
            ref[k // 2, 512:576] = extra


def attn_bwd(me, after, du, gm, y1, x, g1, g2, w, wq, wo, qkv, p, a1, o):
    seqs, length, d = gm.shape
    total = seqs * length
    anys = pl.BlockSpec(memory_space=pl.ANY)
    outs, out_specs = spread_outs(seqs, length // 4, d)
    grads = [struct((2, 576, d), BF16)] * 2
    args = [du, gm, y1, x, g1, g2, w, wq, wo, qkv, p, a1, o, after]
    in_specs = [pl.BlockSpec((length, 4 * d), lambda s, *_: (s, 0)), per_seq(gm), per_seq(y1), per_seq(x), full(g1), full(g2),
                once((4, 1, d, d)), once(wq.shape), once(wo.shape), per_seq(qkv), per_seq(p), once(a1.shape), once(o.shape), anys]
    scratch = [pltpu.VMEM((length, d), BF16), pltpu.VMEM((length, d), F32), pltpu.VMEM((4, length // 4, d), F32),
               pltpu.VMEM((8, d), F32), pltpu.VMEM((1, length, 3 * d), BF16), pltpu.VMEM((total, 3 * d), BF16),
               pltpu.VMEM((total, d), BF16)]
    return call(attn_bwd_kernel, (me,), args, outs + grads, grid=(seqs,), in_specs=in_specs,
                out_specs=out_specs + [once(a.shape) for a in grads], scratch=scratch,
                flops=6 * total * (4 * d * d + 2 * d * length), name="attention_backward", vmem=40 << 20)


def spread(refs, me, full_sc, blk_sc):
    rows = blk_sc.shape[1]
    for i in range(4):
        blk_sc[i] = full_sc[pl.ds(i * rows, rows), :]
    own, near, far = refs
    s = pl.program_id(0)
    each = far.shape[0] // 2
    own[0] = blk_sc[me].astype(BF16)
    near[0] = blk_sc[me ^ 1].astype(BF16)
    far[s] = blk_sc[me ^ 2].astype(BF16)
    far[each + s] = blk_sc[me ^ 3].astype(BF16)


def spread_outs(seqs, rows, d):
    one = struct((seqs, rows, d), BF16)
    far = struct((2 * seqs, rows, d), BF16)
    return [one, one, far], [per_seq(one), per_seq(one), once(far.shape)]


def finish_out_kernel(me_ref, count_ref, hm_ref, w_ref, y1_ref, db_ref, after_ref, o0, o1, o2, full_sc, blk_sc):
    s = pl.program_id(0)
    d = y1_ref.shape[2]
    mlp = None
    for k in range(4):
        part = dot(hm_ref[:, pl.ds(k * d, d)], w_ref[k, 0])
        mlp = part if mlp is None else mlp + part
    full_sc[...] = jnp.where(me_ref[0] * pl.num_programs(0) + s < count_ref[0], y1_ref[0] + mlp + db_ref[...], 0.0)
    spread((o0, o1, o2), me_ref[0], full_sc, blk_sc)


def finish_out(me, count, after, hm, w, y1, db):
    seqs, length, d = y1.shape
    outs, out_specs = spread_outs(seqs, length // 4, d)
    return call(
        finish_out_kernel, (me, count), (hm, w, y1, db, after), outs, grid=(seqs,),
        in_specs=[pl.BlockSpec((length, 4 * d), lambda s, *_: (s, 0)),
                  pl.BlockSpec((4, 1, d, d), lambda s, *_: (0, 1, 0, 0)), per_seq(y1), full(db),
                  pl.BlockSpec(memory_space=pl.ANY)],
        out_specs=out_specs,
        scratch=[pltpu.VMEM((length, d), F32), pltpu.VMEM((4, length // 4, d), F32)],
        flops=2 * seqs * length * 4 * d * d, name="block_output", vmem=56 << 20)


def hop(value, axis, bit):
    n = lax.axis_size(axis)
    return lax.ppermute(value, axis, [(i, i ^ bit) for i in range(n)])


def split(rows, me):
    rows = rows.transpose(1, 0, 2)
    each = rows.shape[0] // 4
    own, near, *far = (lax.dynamic_slice_in_dim(rows, (me ^ k) * each, each) for k in range(4))
    return [own, near, jnp.concatenate(far)]


def exchange(own, near, far):
    far = hop(far, "tensor", 2)
    return [own, hop(near, "tensor", 1), far, far]


def forward(blocks, *after):
    return [*blocks[:3], hop(tie(blocks[3], *after), "tensor", 1)]


def halves(a, side, axis=0):
    n = a.shape[axis] // 2
    return (lax.dynamic_slice_in_dim(a, side * n, n, axis), lax.dynamic_slice_in_dim(a, (1 - side) * n, n, axis))


def join(mine, other, side, axis=0):
    return jnp.where(side == 0, jnp.concatenate([mine, other], axis), jnp.concatenate([other, mine], axis))


def tie(value, *others):
    return lax.optimization_barrier((value, *others))[0]


def plus(a, b):
    return (a.astype(F32) + b.astype(F32)).astype(BF16)


def wait(after, *groups):
    sizes = [len(g) for g in groups]
    flat = lax.optimization_barrier((*[a for g in groups for a in g], *after))
    out = []
    for n in sizes:
        out.append(list(flat[:n]))
        flat = flat[n:]
    return out


class Sum:
    def __init__(self, one, two):
        self.n = lax.axis_size("dp")
        me = lax.axis_index("dp")
        self.one, self.two = one, two
        self.y, self.z = (me // one) % 2, (me // two) % 2

    def step1(self, pair):
        self.middle = middle = pair.shape[1] // 2
        self.a = pair[0, :middle]
        a_other = pair[1, :middle]
        self.b, b_other = halves(pair[:, middle:], self.y, 1)
        self.got = [hop(a_other, "tensor", 2), hop(b_other, "dp", self.one)]
        return [a_other, b_other]

    def step2(self):
        self.a, a_other = halves(plus(self.a, self.got[0]), self.y)
        b = plus(self.b, self.got[1])
        self.b, b_other = b[0], b[1]
        self.got = [hop(a_other, "dp", self.one), hop(b_other, "tensor", 2)]
        return [a_other, b_other]

    def step3(self):
        both = jnp.concatenate([plus(self.a, self.got[0]), plus(self.b, self.got[1])])
        self.part, other = halves(both, self.z)
        self.got = [hop(other, "dp", self.two)]
        return [other]

    def step4(self):
        self.part = plus(self.part, self.got[0])
        top = self.n.bit_length() - 2
        for bit in range(2, top):
            self.part = plus(self.part, hop(self.part, "dp", 1 << bit))
        self.got = [hop(self.part, "dp", 1 << top)]
        return [self.part]

    def step5(self):
        part = plus(self.part, self.got[0])
        n = part.shape[0] // 2
        self.h1, self.h2 = part[:n], part[n:]
        self.got = [hop(self.h1, "dp", self.two), hop(self.h2, "dp", self.one)]
        return [self.h1, self.h2]

    def step6(self):
        pick = lambda mine, other, side: jnp.where(side == 0, jnp.stack([mine, other]), jnp.stack([other, mine]))
        self.h1 = pick(self.h1, self.got[0], self.z)
        self.h2 = pick(self.h2, self.got[1], self.y)
        self.got = [hop(self.h1, "dp", self.one), hop(self.h2, "dp", self.two)]
        return [self.h1, self.h2]

    def result(self):
        pick = lambda mine, other, side, axis: jnp.where(
            side == 0, jnp.stack([mine, other], axis), jnp.stack([other, mine], axis))
        h1 = pick(self.h1, self.got[0], self.y, 1)
        h2 = pick(self.h2, self.got[1], self.z, 0)
        return jnp.concatenate([h1, h2], axis=2).reshape(2 * self.middle, -1)


def shards(
    tokens,
    seq_counts,
    first_frame,
    norm1_gain,
    norm1_bias,
    qkv_weight,
    out_weight,
    out_bias,
    norm2_gain,
    norm2_bias,
    up_weight,
    up_bias,
    down_weight,
    down_bias,
    out_cotangent,
):
    d = tokens.shape[2]
    seqs = tokens.shape[1] // 4
    mine = lax.axis_index("tensor").astype(jnp.int32)
    me = mine.reshape(1)
    y = lax.axis_index("dp").astype(jnp.int32) % 2
    bit = y.reshape(1)
    row = lambda a: a.reshape(1, -1)
    g1, b1, bo, g2, b2, db = map(row, (norm1_gain, norm1_bias, out_bias, norm2_gain, norm2_bias, down_bias))

    z = (lax.axis_index("dp").astype(jnp.int32) // 2) % 2
    zbit = z.reshape(1)
    own, far = pack(bit, zbit, qkv_weight, out_weight, row(up_bias), up_weight, down_weight)
    far_a = hop(far, "tensor", 2)
    near = hop(own, "tensor", 1)
    t = split(tie(tokens, near), mine)
    t_far, t_near = hop(t[2], "tensor", 2), hop(t[1], "tensor", 1)
    cot = split(tie(out_cotangent, t[2]), mine)
    cot_near = hop(cot[1], "tensor", 1)
    far_a = tie(far_a, t_far, t_near, cot[2], cot_near)
    t = [t[0], t_near, t_far, hop(tie(t_far, far_a), "tensor", 1)]
    diag_a = hop(far_a, "tensor", 1)
    far_2 = far_a[d + 32:]
    far_2 = [far_2, hop(far_2, "dp", 2), hop(far_2, "dp", 1), hop(far_2, "dp", 3)]
    w1 = (own, near, far_a, diag_a)
    cot_far = hop(tie(cot[2], t_far), "tensor", 2)

    qkv, p, o, x, y1, a1, a2, wq, wo, ub = attn_fwd(me, first_frame, t, w1, g1, b1, bo, g2, b2)
    near_2 = tie(far_2[1:], a2)
    cot = forward([cot[0], cot_near, cot_far, cot_far], a2)
    w2 = (own, near, far_a, *far_2[1:], diag_a, *(hop(b, "tensor", 1) for b in near_2))
    hm, du, gm, send, keep, w2 = ff(me, bit, zbit, seq_counts, w2, ub, a2, cot)

    m, a = Sum(1, 2), Sum(2, 1)
    got = hop(send, "tensor", 1)
    out = finish_out(me, seq_counts, a2, hm, w2, y1, db)
    ((got,),) = wait(out, [got])
    sent = m.step1(plus(keep, got))
    out = exchange(*tie(out, *sent))
    *dx, send, keep = attn_bwd(me, tie(*sent), du, gm, y1, x, g1, g2, w2, wq, wo, qkv, p, a1, o)
    m.got, out = wait([send], m.got, out[:3])
    out = forward([*out, out[2]])
    sent = m.step2()
    got = hop(tie(send, *sent), "tensor", 1)
    ((got,),) = wait(sent, [got])
    sent = a.step1(plus(keep, got))
    block_output = place(me, tie(out, *sent)).transpose(1, 0, 2)
    (m.got,) = wait([block_output], m.got)
    sent = m.step3()
    (a.got,) = wait(sent, a.got)
    sent = a.step2()
    dx = exchange(*tie(dx, *sent))
    (m.got,) = wait(sent, m.got)
    sent = m.step4()
    (a.got,) = wait(sent, a.got)
    sent = a.step3()
    (m.got,) = wait(sent, m.got)
    sent = m.step5()
    a.got, dx = wait(sent, a.got, dx[:3])
    sent = a.step4()
    dx = forward([*dx, dx[2]], *sent)
    (m.got,) = wait(sent, m.got)
    sent = m.step6()
    input_grad = place(me, tie(dx, *sent)).transpose(1, 0, 2)
    (a.got,) = wait([input_grad], a.got)
    sent = a.step5()
    (m.got,) = wait(sent, m.got)
    mlp_grad = m.result()
    (a.got,) = wait([mlp_grad], a.got)
    a.step6()
    attn_grads = a.result()

    mlp_grad = mlp_grad.astype(F32)
    attn_grads = attn_grads.astype(F32)
    heads = attn_grads[:384].reshape(3, 2, HD, d).transpose(1, 0, 2, 3).reshape(384, d)
    norm2_g, norm2_b, out_b, down_b, norm1_g, norm1_b = (attn_grads[512 + i] for i in range(6))
    return (
        block_output,
        input_grad,
        heads.T,
        attn_grads[384:512],
        mlp_grad[:d],
        mlp_grad[d:2 * d],
        mlp_grad[2 * d],
        out_b,
        down_b,
        norm1_g,
        norm1_b,
        norm2_g,
        norm2_b,
    )


def solution(mesh):
    return jax.shard_map(
        shards,
        mesh=mesh,
        in_specs=(
            P("tensor", "dp", None),
            P("dp"),
            P("dp"),
            P(),
            P(),
            P(None, "tensor"),
            P("tensor", None),
            P(),
            P(),
            P(),
            P(None, "tensor"),
            P("tensor"),
            P("tensor", None),
            P(),
            P("tensor", "dp", None),
        ),
        out_specs=(
            P("tensor", "dp", None),
            P("tensor", "dp", None),
            P(None, "tensor"),
            P("tensor", None),
            P(None, "tensor"),
            P("tensor", None),
            P("tensor"),
            P(),
            P(),
            P(),
            P(),
            P(),
            P(),
        ),
        check_vma=False,
    )
```

```python
import functools
import math

import jax
import jax.numpy as jnp
from jax import lax
from jax.experimental import pallas as pl
from jax.experimental.pallas import tpu as pltpu
from jax.sharding import PartitionSpec as P

HD = 64
FRAME_TOK = 56
BF16 = jnp.bfloat16
F32 = jnp.float32
NN = (((1,), (0,)), ((), ()))
NT = (((1,), (1,)), ((), ()))
TN = (((0,), (0,)), ((), ()))
GELU_A = 0.7978845608
GELU_B = 0.044715
VMEM_LIMIT = 40 << 20


def dot(a, b, dims=NN):
    return lax.dot_general(a, b, dims, preferred_element_type=F32)


def stats(x):
    c = x - jnp.mean(x, axis=-1, keepdims=True)
    inv = lax.rsqrt(jnp.mean(c * c, axis=-1, keepdims=True) + 1e-5)
    return c * inv, inv


def norm_back(d, hat, inv, gain):
    e = d * gain
    return inv * (
        e - jnp.mean(e, axis=-1, keepdims=True) - hat * jnp.mean(e * hat, axis=-1, keepdims=True)
    )


def full(a):
    return pl.BlockSpec(a.shape, lambda *_: (0,) * len(a.shape))


def once(shape, at=None):
    return pl.BlockSpec(shape, lambda *_: at or (0,) * len(shape), pipeline_mode=pl.Buffered(1))


def struct(shape, dtype):
    return jax.ShapeDtypeStruct(shape, dtype)


def call(kernel, scalars, args, out_shape, grid=(1,), in_specs=None, out_specs=None, scratch=(), flops=0, name=None, aliases=None, vmem=VMEM_LIMIT):
    in_specs = [full(a) for a in args] if in_specs is None else in_specs
    out_specs = [full(o) for o in out_shape] if out_specs is None else out_specs
    moved = sum(math.prod(a.shape) * a.dtype.itemsize for a in (*args, *out_shape))
    return pl.pallas_call(
        kernel,
        grid_spec=pltpu.PrefetchScalarGridSpec(
            num_scalar_prefetch=len(scalars),
            grid=grid,
            in_specs=in_specs,
            out_specs=out_specs,
            scratch_shapes=list(scratch),
        ),
        out_shape=list(out_shape),
        compiler_params=pltpu.CompilerParams(vmem_limit_bytes=vmem),
        cost_estimate=pl.CostEstimate(flops=flops, bytes_accessed=moved, transcendentals=0),
        name=name,
        input_output_aliases=aliases or {},
    )(*scalars, *args)


def pack_kernel(y_ref, z_ref, wqkv_ref, wout_ref, ub_ref, up_ref, down_ref, own_ref, far_ref):
    d = wout_ref.shape[1]
    half = d // 2
    pitch = half + 16
    ub = ub_ref[...]
    high = ub.astype(BF16).astype(F32)
    row = lax.broadcasted_iota(jnp.int32, (16, d), 0)
    ub = jnp.where(row == 0, high, jnp.where(row == 1, ub - high, 0.0)).astype(BF16)
    side = wout_ref.shape[0]
    for h in range(2):
        here = pl.ds(h * half, half)
        there = pl.ds(h * pitch, half)
        a, b, c = (wqkv_ref[here, pl.ds(128 * j, 128)].astype(F32) for j in range(3))
        low = lax.broadcasted_iota(jnp.int32, a.shape, 1) < HD
        own_ref[there, 0:128] = jnp.where(low, a, b).astype(BF16)
        own_ref[there, 128:256] = pltpu.roll(jnp.where(low, c, a), HD, 1).astype(BF16)
        own_ref[there, 256:384] = jnp.where(low, b, c).astype(BF16)
        for j in range(half // side):
            own_ref[pl.ds(h * pitch + j * side, side), 384:512] = wout_ref[:, pl.ds(h * half + 128 * j, 128)]
        own_ref[pl.ds(h * pitch + half, 16), :] = ub
    own_ref[2 * pitch:2 * pitch + d] = up_ref[...]
    own_ref[2 * pitch + d:2 * pitch + 2 * d] = down_ref[...]
    far_ref[0:2 * pitch] = own_ref[0:2 * pitch]
    at = 2 * pitch + y_ref[0] * d + z_ref[0] * half
    far_ref[2 * pitch:] = own_ref[pl.ds(pl.multiple_of(at, 16), half)]


def pack(y, z, wqkv, wout, ub, up, down):
    d = wqkv.shape[0]
    half = d // 2
    return call(pack_kernel, (y, z), (wqkv, wout, ub, up, down),
                [struct((3 * d + 32, d), BF16), struct((d + half + 32, d), BF16)], name="pack_weights", vmem=56 << 20)


def place_kernel(me_ref, b0, b1, b2, b3, out_ref):
    each = b0.shape[0]
    for k, b in enumerate((b0, b1, b2, b3)):
        out_ref[pl.ds((me_ref[0] ^ k) * each, each)] = b[...]


def far_specs(a):
    return [pl.BlockSpec((a.shape[0] // 2, *a.shape[1:]), lambda *_, n=n: (n, 0, 0)) for n in range(2)]


def far_seq_specs(a):
    return [pl.BlockSpec((1, *a.shape[1:]), lambda s, *_, n=n: (n * (a.shape[0] // 2) + s, 0, 0)) for n in range(2)]


def place(me, blocks):
    each, rows, d = blocks[0].shape
    return call(place_kernel, (me,), blocks, [struct((4 * each, rows, d), BF16)],
                in_specs=[full(blocks[0]), full(blocks[1])] + far_specs(blocks[2]), name="place")[0]


def attn_fwd_kernel(me_ref, ff_ref, t0, t1, t2, t3, w0, w1, w2, w3,
                    g1_ref, b1_ref, bo_ref, g2_ref, b2_ref,
                    qkv_ref, p_ref, o_ref, x_ref, y1_ref, a1_ref, a2_ref, wq_ref, wo_ref, ub_ref,
                    blk_sc, bias_sc, x_sc):
    s = pl.program_id(0)
    _, rows, d = t0.shape
    length = 4 * rows
    me = me_ref[0]

    @pl.when(s == 0)
    def _():
        half = d // 2
        pitch = half + 16
        for k, w in enumerate((w0, w1, w2, w3)):
            for h in range(2):
                q_cols = w[pl.ds(h * pitch, half), 0:128].astype(F32) * (HD ** -0.5)
                wq_ref[pl.ds(h * half, half), pl.ds(384 * k, 128)] = q_cols.astype(BF16)
                wq_ref[pl.ds(h * half, half), pl.ds(384 * k + 128, 256)] = w[pl.ds(h * pitch, half), 128:384]
                for j in range(half // 128):
                    wo_ref[pl.ds(128 * k, 128), pl.ds(h * half + 128 * j, 128)] = w[pl.ds(h * pitch + 128 * j, 128), 384:512]
            ub = w[half:pitch, :].astype(F32)
            ub_ref[k] = jnp.broadcast_to(ub[0:1] + ub[1:2], ub_ref.shape[1:])

    for k, t in enumerate((t0, t1, t2, t3)):
        blk_sc[me ^ k] = t[0].astype(F32)
    for i in range(4):
        x_sc[pl.ds(i * rows, rows), :] = blk_sc[i]
    x_ref[0] = x_sc[...].astype(BF16)
    hat, _ = stats(x_sc[...])
    a1 = (hat * g1_ref[...] + b1_ref[...]).astype(BF16)
    a1_ref[0] = a1
    qkv_ref[0] = dot(a1, wq_ref[...]).astype(BF16)
    start = ff_ref[me * pl.num_programs(0) + s] * FRAME_TOK
    jj = lax.broadcasted_iota(jnp.int32, (length, length), 0)
    ii = lax.broadcasted_iota(jnp.int32, (length, length), 1)
    bias_sc[...] = jnp.where((jj <= ii) & ((jj >= start) | (jj == ii)), 0.0, -1e30)
    lane = lax.broadcasted_iota(jnp.int32, (length, 128), 1)
    for p in range(4):
        q = qkv_ref[0, :, pl.ds(p * 384, 128)]
        k = qkv_ref[0, :, pl.ds(p * 384 + 128, 128)]
        v = qkv_ref[0, :, pl.ds(p * 384 + 256, 128)]
        acc = None
        for h in range(2):
            mine = (lane < HD) if h == 0 else (lane >= HD)
            kh = jnp.where(mine, k, jnp.zeros_like(k))
            vh = jnp.where(mine, v, jnp.zeros_like(v))
            st = dot(kh, q, NT) + bias_sc[...]
            e = jnp.exp(st - jnp.max(st, axis=0, keepdims=True))
            prob = (e * (1.0 / jnp.sum(e, axis=0, keepdims=True))).astype(BF16)
            p_ref[0, 2 * p + h] = prob
            part = dot(prob, vh, TN)
            acc = part if acc is None else acc + part
        o_ref[0, :, pl.ds(p * 128, 128)] = acc.astype(BF16)
    y1 = x_sc[...] + dot(o_ref[0], wo_ref[...]) + bo_ref[...]
    y1_ref[0] = y1
    hat, _ = stats(y1)
    a2_ref[0] = (hat * g2_ref[...] + b2_ref[...]).astype(BF16)


def per_seq(a):
    return pl.BlockSpec((1, *a.shape[1:]), lambda s, *_: (s,) + (0,) * (len(a.shape) - 1))


def attn_fwd(me, ff, t, w, g1, b1, bo, g2, b2):
    seqs, rows, d = t[0].shape
    length = 4 * rows
    small = (g1, b1, bo, g2, b2)
    outs = [
        struct((seqs, length, 3 * d), BF16),
        struct((seqs, 8, length, length), BF16),
        struct((seqs, length, d), BF16),
        struct((seqs, length, d), BF16),
        struct((seqs, length, d), F32),
        struct((seqs, length, d), BF16),
        struct((seqs, length, d), BF16),
    ]
    weights = [struct((d, 3 * d), BF16), struct((d, d), BF16), struct((4, 8, d), F32)]
    return call(
        attn_fwd_kernel, (me, ff), (*t, *w, *small), outs + weights, grid=(seqs,),
        in_specs=[per_seq(a) for a in t[:2]] + far_seq_specs(t[2]) + [pl.BlockSpec((d + 32, d), lambda *_: (0, 0))] * 4 + [full(a) for a in small],
        out_specs=[per_seq(o) for o in outs] + [full(o) for o in weights],
        scratch=[pltpu.VMEM((4, rows, d), F32), pltpu.VMEM((length, length), F32), pltpu.VMEM((length, d), F32)],
        flops=2 * seqs * length * (4 * d * d + 2 * d * length), name="attention_forward", vmem=56 << 20)


def ff_kernel(me_ref, y_ref, z_ref, count_ref, w0, w1, a2_, b2_, c2_, d2_, a3_, b3_, c3_, d3_, ub_ref, a2_ref, c0, c1, c2, c3,
              hm_ref, du_ref, gm_ref, send_ref, keep_ref, w_ref, wbuf, sems, out_sems, blk_sc, row_sc):
    c = pl.program_id(0)
    seqs, length, d = a2_ref.shape
    total = seqs * length
    y, z = y_ref[0], z_ref[0]
    half = d // 2
    pitch = half + 16
    quarter = lambda k, at, side: wbuf.at[k, at, pl.ds(pl.multiple_of(side * half, half), half)]
    copies = [
        [pltpu.make_async_copy(w.at[pl.ds(2 * pitch + n * d, d)], wbuf.at[k, n], sems.at[k, n]) for n in range(2)]
        for k, w in enumerate((w0, w1))
    ] + [
        [pltpu.make_async_copy(a.at[pl.ds(2 * pitch, half)], quarter(k, y, z), sems.at[k, 0]),
         pltpu.make_async_copy(b, quarter(k, y, 1 - z), sems.at[k, 1]),
         pltpu.make_async_copy(c, quarter(k, 1 - y, z), sems.at[k, 2]),
         pltpu.make_async_copy(e, quarter(k, 1 - y, 1 - z), sems.at[k, 3])]
        for k, (a, b, c, e) in ((2, (a2_, b2_, c2_, d2_)), (3, (a3_, b3_, c3_, d3_)))
    ]
    out_copies = [pltpu.make_async_copy(wbuf.at[k], w_ref.at[k], out_sems.at[k]) for k in range(4)]
    order = (3, 1, 2, 0)

    @pl.when(c == 0)
    def _():
        for k in order:
            for cp in copies[k]:
                cp.start()
        rows = length // 4
        for s in range(seqs):
            live = me_ref[0] * seqs + s < count_ref[0]
            for k, cot in enumerate((c0, c1, c2, c3)):
                blk_sc[me_ref[0] ^ k] = jnp.where(live, cot[s].astype(F32), 0.0)
            for i in range(4):
                row_sc[pl.ds(i * rows, rows), :] = blk_sc[i]
            gm_ref[s] = row_sc[...].astype(BF16)

    for n, k in enumerate(order):
        @pl.when(c == n)
        def _():
            for cp in copies[k]:
                cp.wait()
            out_copies[k].start()

    blk = jnp.where(c == 0, 3, jnp.where(c == 1, 1, jnp.where(c == 2, 2, 0)))
    up = wbuf[blk, 0]
    dn = wbuf[blk, 1]
    ub = ub_ref[blk, 0:1]
    ubg = jnp.zeros((8, d), F32)
    for s in range(seqs):
        here = pl.ds(s * length, length)
        pre = dot(a2_ref[s], up) + ub
        dh = dot(gm_ref[s], dn, NT)
        sq = pre * pre
        t = jnp.tanh(pre * (GELU_A + (GELU_A * GELU_B) * sq))
        ht = 0.5 * t + 0.5
        slope = ht + (ht - ht * ht) * (pre * ((2 * GELU_A) + (6.0 * GELU_A * GELU_B) * sq))
        hm_ref[here, :] = (pre * ht).astype(BF16)
        du = (dh * slope).astype(BF16)
        du_ref[here, :] = du
        ubg += jnp.sum(du.astype(F32).reshape(length // 8, 8, d), axis=0)
    upg = dot(a2_ref[...].reshape(total, d), du_ref[...], TN).astype(BF16)
    dng = dot(hm_ref[...], gm_ref[...].reshape(total, d), TN).astype(BF16)
    ubg = jnp.sum(ubg, axis=0, keepdims=True)
    extra = jnp.where(lax.broadcasted_iota(jnp.int32, (64, d), 0) == 0, ubg, 0.0).astype(BF16)

    @pl.when(c < 2)
    def _():
        send_ref[0, 0:d, :] = upg
        send_ref[0, d:2 * d, :] = dng
        send_ref[0, 2 * d:2 * d + 64, :] = extra

    @pl.when(c >= 2)
    def _():
        keep_ref[0, 0:d, :] = upg
        keep_ref[0, d:2 * d, :] = dng
        keep_ref[0, 2 * d:2 * d + 64, :] = extra

    @pl.when(c == 3)
    def _():
        for cp in out_copies:
            cp.wait()


def ff(me, y, z, count, w, ub, a2, cots):
    seqs, length, d = a2.shape
    total = seqs * length
    anys = pl.BlockSpec(memory_space=pl.ANY)
    column = lambda c, *_: (0, jnp.where(c == 0, 3, jnp.where(c == 1, 1, jnp.where(c == 2, 2, 0))))
    outs = [struct((total, 4 * d), BF16)] * 2 + [struct((seqs, length, d), BF16)] + [
        struct((2, 2 * d + 64, d), BF16)] * 2 + [struct((4, 2, d, d), BF16)]
    return call(
        ff_kernel, (me, y, z, count), (*w, ub, a2, *cots), outs, grid=(4,),
        in_specs=[anys] * 10 + [full(a) for a in (ub, a2, *cots[:2])] + far_specs(cots[2]),
        out_specs=[pl.BlockSpec((total, d), column)] * 2 + [
            full(outs[2]),
            pl.BlockSpec((1, 2 * d + 64, d), lambda c, *_: (1 - jnp.minimum(c, 1), 0, 0)),
            pl.BlockSpec((1, 2 * d + 64, d), lambda c, *_: (1 - jnp.maximum(c - 2, 0), 0, 0)),
            anys],
        scratch=[pltpu.VMEM((4, 2, d, d), BF16), pltpu.SemaphoreType.DMA((4, 4)), pltpu.SemaphoreType.DMA((4,)),
                 pltpu.VMEM((4, length // 4, d), F32), pltpu.VMEM((length, d), F32)],
        flops=16 * total * d * d, name="feed_forward", vmem=50 << 20)


def attn_bwd_kernel(me_ref, du_ref, gm_ref, y1_ref, x_ref, g1_ref, g2_ref, w_ref, wq_ref, wo_ref, qkv_ref, p_ref,
                    a1_ref, o_ref, after_ref, d0, d1, d2, send_ref, keep_ref,
                    do_sc, full_sc, blk_sc, small_ref, dqkv_ref, dqkv_sc, ga_sc):
    dxs = (d0, d1, d2)
    s = pl.program_id(0)
    _, length, d = gm_ref.shape
    here = pl.ds(pl.multiple_of(s * length, 16), length)

    @pl.when(s == 0)
    def _():
        small_ref[...] = jnp.zeros_like(small_ref)

    da2 = None
    for k in range(4):
        part = dot(du_ref[:, pl.ds(k * d, d)], w_ref[k, 0], NT)
        da2 = part if da2 is None else da2 + part
    hat, inv = stats(y1_ref[0])
    gy = gm_ref[0].astype(F32)
    dy1 = gy + norm_back(da2, hat, inv, g2_ref[...])
    full_sc[...] = dy1
    ga = dy1.astype(BF16)
    ga_sc[here, :] = ga
    sums = [jnp.sum(v, axis=0, keepdims=True) for v in (da2 * hat, da2, ga.astype(F32), gy)]
    do_sc[...] = dot(ga, wo_ref[...], NT).astype(BF16)
    lane = lax.broadcasted_iota(jnp.int32, (length, 128), 1)
    cut = min(256, length)
    for p in range(4):
        q = qkv_ref[0, :, pl.ds(p * 384, 128)]
        k = qkv_ref[0, :, pl.ds(p * 384 + 128, 128)]
        v = qkv_ref[0, :, pl.ds(p * 384 + 256, 128)]
        do = do_sc[:, pl.ds(p * 128, 128)]
        for h in range(2):
            mine = (lane < HD) if h == 0 else (lane >= HD)
            zero = jnp.zeros_like(q)
            qh, kh, vh, doh = (jnp.where(mine, a, zero) for a in (q, k, v, do))
            prob = p_ref[0, 2 * p + h]
            dp = dot(vh, do, NT)
            probs = prob.astype(F32)
            pd = probs * dp
            ds = (pd - probs * jnp.sum(pd, axis=0, keepdims=True)).astype(BF16)
            pq = dot(ds[:cut, :cut], kh[:cut], TN), dot(ds[:, cut:], kh, TN)
            pk = dot(ds[:cut], qh), dot(ds[cut:, cut:], qh[cut:])
            pv = dot(prob[:cut], doh), dot(prob[cut:, cut:], doh[cut:])
            parts = (pq, pk, pv)
            total = parts if h == 0 else [[b + c for b, c in zip(*pair)] for pair in zip(total, parts)]
        for n, kind in enumerate(total):
            for rows, value in zip((pl.ds(0, cut), pl.ds(cut, length - cut)), kind):
                dqkv_ref[0, rows, pl.ds(p * 384 + 128 * n, 128)] = value.astype(BF16)

    da1 = dot(dqkv_ref[0], wq_ref[...], NT)
    hat, inv = stats(x_ref[0].astype(F32))
    sums += [jnp.sum(v, axis=0, keepdims=True) for v in (da1 * hat, da1)]
    full_sc[...] += norm_back(da1, hat, inv, g1_ref[...])
    spread(dxs, me_ref[0], full_sc, blk_sc)
    row = lax.broadcasted_iota(jnp.int32, (8, d), 0)
    small = jnp.zeros((8, d), F32)
    for n, v in enumerate(sums):
        small = jnp.where(row == n, v, small)
    small_ref[...] += small


    dqkv_sc[here, :] = dqkv_ref[0]

    @pl.when(s == pl.num_programs(0) - 1)
    def _():
        total = dqkv_sc.shape[0]
        extra = jnp.concatenate([small_ref[...], jnp.zeros((56, d), F32)], axis=0).astype(BF16)
        for k in range(4):
            ref = send_ref if k % 2 else keep_ref
            grad = dot(dqkv_sc[:, pl.ds(384 * k, 384)], a1_ref[...].reshape(total, d), TN)
            ref[k // 2, 0:128] = (grad[0:128] * (HD ** -0.5)).astype(BF16)
            ref[k // 2, 128:384] = grad[128:384].astype(BF16)
            ref[k // 2, 384:512] = dot(o_ref[:, :, pl.ds(128 * k, 128)].reshape(total, 128), ga_sc[...], TN).astype(BF16)
            ref[k // 2, 512:576] = extra


def attn_bwd(me, after, du, gm, y1, x, g1, g2, w, wq, wo, qkv, p, a1, o):
    seqs, length, d = gm.shape
    total = seqs * length
    anys = pl.BlockSpec(memory_space=pl.ANY)
    outs, out_specs = spread_outs(seqs, length // 4, d)
    grads = [struct((2, 576, d), BF16)] * 2
    args = [du, gm, y1, x, g1, g2, w, wq, wo, qkv, p, a1, o, after]
    in_specs = [pl.BlockSpec((length, 4 * d), lambda s, *_: (s, 0)), per_seq(gm), per_seq(y1), per_seq(x), full(g1), full(g2),
                once((4, 1, d, d)), once(wq.shape), once(wo.shape), per_seq(qkv), per_seq(p), once(a1.shape), once(o.shape), anys]
    scratch = [pltpu.VMEM((length, d), BF16), pltpu.VMEM((length, d), F32), pltpu.VMEM((4, length // 4, d), F32),
               pltpu.VMEM((8, d), F32), pltpu.VMEM((1, length, 3 * d), BF16), pltpu.VMEM((total, 3 * d), BF16),
               pltpu.VMEM((total, d), BF16)]
    return call(attn_bwd_kernel, (me,), args, outs + grads, grid=(seqs,), in_specs=in_specs,
                out_specs=out_specs + [once(a.shape) for a in grads], scratch=scratch,
                flops=6 * total * (4 * d * d + 2 * d * length), name="attention_backward", vmem=40 << 20)


def spread(refs, me, full_sc, blk_sc):
    rows = blk_sc.shape[1]
    for i in range(4):
        blk_sc[i] = full_sc[pl.ds(i * rows, rows), :]
    own, near, far = refs
    s = pl.program_id(0)
    each = far.shape[0] // 2
    own[0] = blk_sc[me].astype(BF16)
    near[0] = blk_sc[me ^ 1].astype(BF16)
    far[s] = blk_sc[me ^ 2].astype(BF16)
    far[each + s] = blk_sc[me ^ 3].astype(BF16)


def spread_outs(seqs, rows, d):
    one = struct((seqs, rows, d), BF16)
    far = struct((2 * seqs, rows, d), BF16)
    return [one, one, far], [per_seq(one), per_seq(one), once(far.shape)]


def finish_out_kernel(me_ref, count_ref, hm_ref, w_ref, y1_ref, db_ref, after_ref, o0, o1, o2, full_sc, blk_sc):
    s = pl.program_id(0)
    d = y1_ref.shape[2]
    mlp = None
    for k in range(4):
        part = dot(hm_ref[:, pl.ds(k * d, d)], w_ref[k, 0])
        mlp = part if mlp is None else mlp + part
    full_sc[...] = jnp.where(me_ref[0] * pl.num_programs(0) + s < count_ref[0], y1_ref[0] + mlp + db_ref[...], 0.0)
    spread((o0, o1, o2), me_ref[0], full_sc, blk_sc)


def finish_out(me, count, after, hm, w, y1, db):
    seqs, length, d = y1.shape
    outs, out_specs = spread_outs(seqs, length // 4, d)
    return call(
        finish_out_kernel, (me, count), (hm, w, y1, db, after), outs, grid=(seqs,),
        in_specs=[pl.BlockSpec((length, 4 * d), lambda s, *_: (s, 0)),
                  pl.BlockSpec((4, 1, d, d), lambda s, *_: (0, 1, 0, 0)), per_seq(y1), full(db),
                  pl.BlockSpec(memory_space=pl.ANY)],
        out_specs=out_specs,
        scratch=[pltpu.VMEM((length, d), F32), pltpu.VMEM((4, length // 4, d), F32)],
        flops=2 * seqs * length * 4 * d * d, name="block_output", vmem=56 << 20)


def hop(value, axis, bit):
    n = lax.axis_size(axis)
    return lax.ppermute(value, axis, [(i, i ^ bit) for i in range(n)])


def split(rows, me):
    rows = rows.transpose(1, 0, 2)
    each = rows.shape[0] // 4
    own, near, *far = (lax.dynamic_slice_in_dim(rows, (me ^ k) * each, each) for k in range(4))
    return [own, near, jnp.concatenate(far)]


def exchange(own, near, far):
    far = hop(far, "tensor", 2)
    return [own, hop(near, "tensor", 1), far, far]


def forward(blocks, *after):
    return [*blocks[:3], hop(tie(blocks[3], *after), "tensor", 1)]


def halves(a, side, axis=0):
    n = a.shape[axis] // 2
    return (lax.dynamic_slice_in_dim(a, side * n, n, axis), lax.dynamic_slice_in_dim(a, (1 - side) * n, n, axis))


def join(mine, other, side, axis=0):
    return jnp.where(side == 0, jnp.concatenate([mine, other], axis), jnp.concatenate([other, mine], axis))


def tie(value, *others):
    return lax.optimization_barrier((value, *others))[0]


def plus(a, b):
    return (a.astype(F32) + b.astype(F32)).astype(BF16)


def wait(after, *groups):
    sizes = [len(g) for g in groups]
    flat = lax.optimization_barrier((*[a for g in groups for a in g], *after))
    out = []
    for n in sizes:
        out.append(list(flat[:n]))
        flat = flat[n:]
    return out


class Sum:
    def __init__(self, one, two):
        self.n = lax.axis_size("dp")
        me = lax.axis_index("dp")
        self.one, self.two = one, two
        self.y, self.z = (me // one) % 2, (me // two) % 2

    def step1(self, pair):
        self.middle = middle = pair.shape[1] // 2
        self.a = pair[0, :middle]
        a_other = pair[1, :middle]
        self.b, b_other = halves(pair[:, middle:], self.y, 1)
        self.got = [hop(a_other, "tensor", 2), hop(b_other, "dp", self.one)]
        return [a_other, b_other]

    def step2(self):
        self.a, a_other = halves(plus(self.a, self.got[0]), self.y)
        b = plus(self.b, self.got[1])
        self.b, b_other = b[0], b[1]
        self.got = [hop(a_other, "dp", self.one), hop(b_other, "tensor", 2)]
        return [a_other, b_other]

    def step3(self):
        both = jnp.concatenate([plus(self.a, self.got[0]), plus(self.b, self.got[1])])
        self.part, other = halves(both, self.z)
        self.got = [hop(other, "dp", self.two)]
        return [other]

    def step4(self):
        self.part = plus(self.part, self.got[0])
        top = self.n.bit_length() - 2
        for bit in range(2, top):
            self.part = plus(self.part, hop(self.part, "dp", 1 << bit))
        self.got = [hop(self.part, "dp", 1 << top)]
        return [self.part]

    def step5(self):
        part = plus(self.part, self.got[0])
        n = part.shape[0] // 2
        self.h1, self.h2 = part[:n], part[n:]
        self.got = [hop(self.h1, "dp", self.two), hop(self.h2, "dp", self.one)]
        return [self.h1, self.h2]

    def step6(self):
        pick = lambda mine, other, side: jnp.where(side == 0, jnp.stack([mine, other]), jnp.stack([other, mine]))
        self.h1 = pick(self.h1, self.got[0], self.z)
        self.h2 = pick(self.h2, self.got[1], self.y)
        self.got = [hop(self.h1, "dp", self.one), hop(self.h2, "dp", self.two)]
        return [self.h1, self.h2]

    def result(self):
        pick = lambda mine, other, side, axis: jnp.where(
            side == 0, jnp.stack([mine, other], axis), jnp.stack([other, mine], axis))
        h1 = pick(self.h1, self.got[0], self.y, 1)
        h2 = pick(self.h2, self.got[1], self.z, 0)
        return jnp.concatenate([h1, h2], axis=2).reshape(2 * self.middle, -1)


def shards(
    tokens,
    seq_counts,
    first_frame,
    norm1_gain,
    norm1_bias,
    qkv_weight,
    out_weight,
    out_bias,
    norm2_gain,
    norm2_bias,
    up_weight,
    up_bias,
    down_weight,
    down_bias,
    out_cotangent,
):
    d = tokens.shape[2]
    seqs = tokens.shape[1] // 4
    mine = lax.axis_index("tensor").astype(jnp.int32)
    me = mine.reshape(1)
    y = lax.axis_index("dp").astype(jnp.int32) % 2
    bit = y.reshape(1)
    row = lambda a: a.reshape(1, -1)
    g1, b1, bo, g2, b2, db = map(row, (norm1_gain, norm1_bias, out_bias, norm2_gain, norm2_bias, down_bias))

    z = (lax.axis_index("dp").astype(jnp.int32) // 2) % 2
    zbit = z.reshape(1)
    own, far = pack(bit, zbit, qkv_weight, out_weight, row(up_bias), up_weight, down_weight)
    far_a = hop(far, "tensor", 2)
    near = hop(own, "tensor", 1)
    t = split(tie(tokens, near), mine)
    t_far, t_near = hop(t[2], "tensor", 2), hop(t[1], "tensor", 1)
    cot = split(tie(out_cotangent, t[2]), mine)
    cot_near = hop(cot[1], "tensor", 1)
    far_a = tie(far_a, t_far, t_near, cot[2], cot_near)
    t = [t[0], t_near, t_far, hop(tie(t_far, far_a), "tensor", 1)]
    diag_a = hop(far_a, "tensor", 1)
    far_2 = far_a[d + 32:]
    far_2 = [far_2, hop(far_2, "dp", 2), hop(far_2, "dp", 1), hop(far_2, "dp", 3)]
    w1 = (own, near, far_a, diag_a)
    cot_far = hop(tie(cot[2], t_far), "tensor", 2)

    qkv, p, o, x, y1, a1, a2, wq, wo, ub = attn_fwd(me, first_frame, t, w1, g1, b1, bo, g2, b2)
    near_2 = tie(far_2[1:], a2)
    cot = forward([cot[0], cot_near, cot_far, cot_far], a2)
    w2 = (own, near, far_a, *far_2[1:], diag_a, *(hop(b, "tensor", 1) for b in near_2))
    hm, du, gm, send, keep, w2 = ff(me, bit, zbit, seq_counts, w2, ub, a2, cot)

    m, a = Sum(1, 2), Sum(2, 1)
    got = hop(send, "tensor", 1)
    out = finish_out(me, seq_counts, a2, hm, w2, y1, db)
    ((got,),) = wait(out, [got])
    sent = m.step1(plus(keep, got))
    out = exchange(*tie(out, *sent))
    *dx, send, keep = attn_bwd(me, tie(*sent), du, gm, y1, x, g1, g2, w2, wq, wo, qkv, p, a1, o)
    m.got, out = wait([send], m.got, out[:3])
    out = forward([*out, out[2]])
    sent = m.step2()
    got = hop(tie(send, *sent), "tensor", 1)
    ((got,),) = wait(sent, [got])
    sent = a.step1(plus(keep, got))
    block_output = place(me, tie(out, *sent)).transpose(1, 0, 2)
    (m.got,) = wait([block_output], m.got)
    sent = m.step3()
    (a.got,) = wait(sent, a.got)
    sent = a.step2()
    dx = exchange(*tie(dx, *sent))
    (m.got,) = wait(sent, m.got)
    sent = m.step4()
    (a.got,) = wait(sent, a.got)
    sent = a.step3()
    (m.got,) = wait(sent, m.got)
    sent = m.step5()
    a.got, dx = wait(sent, a.got, dx[:3])
    sent = a.step4()
    dx = forward([*dx, dx[2]], *sent)
    (m.got,) = wait(sent, m.got)
    sent = m.step6()
    input_grad = place(me, tie(dx, *sent)).transpose(1, 0, 2)
    (a.got,) = wait([input_grad], a.got)
    sent = a.step5()
    (m.got,) = wait(sent, m.got)
    mlp_grad = m.result()
    (a.got,) = wait([mlp_grad], a.got)
    a.step6()
    attn_grads = a.result()

    mlp_grad = mlp_grad.astype(F32)
    attn_grads = attn_grads.astype(F32)
    heads = attn_grads[:384].reshape(3, 2, HD, d).transpose(1, 0, 2, 3).reshape(384, d)
    norm2_g, norm2_b, out_b, down_b, norm1_g, norm1_b = (attn_grads[512 + i] for i in range(6))
    return (
        block_output,
        input_grad,
        heads.T,
        attn_grads[384:512],
        mlp_grad[:d],
        mlp_grad[d:2 * d],
        mlp_grad[2 * d],
        out_b,
        down_b,
        norm1_g,
        norm1_b,
        norm2_g,
        norm2_b,
    )


def solution(mesh):
    return jax.shard_map(
        shards,
        mesh=mesh,
        in_specs=(
            P("tensor", "dp", None),
            P("dp"),
            P("dp"),
            P(),
            P(),
            P(None, "tensor"),
            P("tensor", None),
            P(),
            P(),
            P(),
            P(None, "tensor"),
            P("tensor"),
            P("tensor", None),
            P(),
            P("tensor", "dp", None),
        ),
        out_specs=(
            P("tensor", "dp", None),
            P("tensor", "dp", None),
            P(None, "tensor"),
            P("tensor", None),
            P(None, "tensor"),
            P("tensor", None),
            P("tensor"),
            P(),
            P(),
            P(),
            P(),
            P(),
            P(),
        ),
        check_vma=False,
    )
```
